32 devices in a mesh: outer: 16 (over z, y, core), inner: 2 (over x).
Axes of the slice: x: 2, y: 2, z: 4, core: 2. Of those that a mesh axis runs over, the one named last changes fastest.
Arguments:
- queries: bfloat16 [4096, 1024], P(('outer', 'inner')), may hold values from -9 to 9
- keys: bfloat16 [4096, 128], P(('outer', 'inner')), may hold values from -9 to 9
- values: bfloat16 [4096, 128], P(('outer', 'inner')), may hold values from -6 to 6
- grad_out: bfloat16 [4096, 1024], P(('outer', 'inner')), may hold values from -6 to 6
- doc_lengths: int32 [16], replicated, may hold values from 1 to 1024, 4096 in all
Outputs:
- grad_queries: bfloat16 [4096, 1024], P(('outer', 'inner'))
- grad_keys: bfloat16 [4096, 128], P(('outer', 'inner'))
- grad_values: bfloat16 [4096, 128], P(('outer', 'inner'))
The draws below stay inside these ranges and needn't reach their ends.
Inputs may be any that keep to these rules, and one draw needn't show every extreme that they name: `doc_lengths`: the lengths sum to 4096; the longest document has exactly 1024 tokens.
All inputs are finite; a program needn't handle non-finite values.
Results may differ from the reference program's by a relative error of at most 0.0074.
Values may be sent and summed in bfloat16 or wider, within the bound.
No kernel may reach another device: no remote copies, remote signals or barrier semaphores. Data moves between devices by JAX's collectives and lax.ppermute only.
A program may use at most 128 MiB of HBM per device.

```python
import math
import jax
import jax.numpy as jnp
import numpy as np
from jax import lax

HEADS = 8
HEAD_DIM = 128
TOK_DEV = 128
REACH = 4
DOCS = 16
SEQ = 4096
MOST = 1024
N_OUTER = 16
N_INNER = 2


def draw_queries(key, part):
    key = jax.random.fold_in(key, 1)
    result = jnp.clip(jax.random.normal(key, (SEQ, HEADS * HEAD_DIM), jnp.float32), -6.0, 6.0)
    return result.astype(jnp.bfloat16)


def draw_keys(key, part):
    key = jax.random.fold_in(key, 2)
    result = jnp.clip(jax.random.normal(key, (SEQ, HEAD_DIM), jnp.float32), -6.0, 6.0)
    return result.astype(jnp.bfloat16)


def block_scale(own_key, extent, pieces, least, top_value):
    gain, own = 1.0, jax.random.fold_in(own_key, 6)
    for axis_at, shards_of in pieces:
        heights = jnp.exp(jax.random.uniform(jax.random.fold_in(own, axis_at), (shards_of,), jnp.float32, least / len(pieces), top_value / len(pieces)))
        gain = gain * jnp.repeat(heights, extent[axis_at] // shards_of).reshape([-1 if axis == axis_at else 1 for axis in range(len(extent))])
    return gain


def profile(count, total, most, skew):
    weights = [(1 << 20) // math.isqrt(rank ** skew) + 1 for rank in range(2, count + 1)]
    rest, given = total - most - (count - 1), [1] * (count - 1)
    while rest > 0:
        candidates = [i for i in range(count - 1) if given[i] < most]
        mass, budget = sum([weights[i] for i in candidates]), rest
        for i in candidates:
            extra = min(most - given[i], max(1, budget * weights[i] // mass), rest)
            given[i] = given[i] + extra
            rest = rest - extra
    return np.array([most] + given)


def ragged(rng, amount, total, limit, lean):
    if amount == 2:
        one = jax.random.randint(rng, (), max(1, total - limit), min(limit, total - 1) + 1)
        return jnp.stack([one, total - one])
    lengths = jnp.asarray(profile(amount, total, limit, lean), jnp.int32)
    couples = (amount - 1) // 2
    source_of, receiver = lengths[1:1 + 2 * couples:2], lengths[2:2 + 2 * couples:2]
    room = jnp.minimum(source_of - 1, limit - receiver)
    moved = jax.random.randint(jax.random.fold_in(rng, 1), (couples,), 0, 1 << 20) % (room + 1)
    lengths = lengths.at[1:1 + 2 * couples:2].set(source_of - moved).at[2:2 + 2 * couples:2].set(receiver + moved)
    return lengths[jax.random.permutation(jax.random.fold_in(rng, 2), amount)]


def centred(key, shape, scale, limit, split=(), kind=jnp.bfloat16):
    drawn = scale * jax.random.normal(key, shape, jnp.float32)
    if split:
        drawn = drawn * block_scale(key, shape, split, -0.22, 0.18)
    return jnp.clip(drawn, -limit, limit).astype(kind)


def setup_inputs(seed: int = 0) -> dict:
    key_list = jax.random.split(jax.random.key(seed), 6)
    queries = draw_queries(jax.random.fold_in(key_list[5], 71), 0)
    keys = draw_keys(jax.random.fold_in(key_list[5], 71), 0)
    values = centred(key_list[2], (SEQ, HEAD_DIM), 1.0, 6.0, ((0, 32),))
    grad_out = centred(key_list[3], (SEQ, HEADS * HEAD_DIM), 1.0, 6.0, ((0, 32),))
    doc_lengths = ragged(key_list[4], DOCS, SEQ, MOST, 2).astype(jnp.int32)
    return {"queries": queries, "keys": keys, "values": values, "grad_out": grad_out, "doc_lengths": doc_lengths}


NEG = -1e+30

def doc_of(positions, doc_lengths):
    ends = jnp.cumsum(doc_lengths)
    return lax.optimization_barrier(jnp.sum((positions[:, None] >= ends[None, :]).astype(jnp.int32), axis=1))

def allowed(query_pos, key_pos, doc_lengths):
    same = doc_of(query_pos, doc_lengths)[:, None] == doc_of(key_pos, doc_lengths)[None, :]
    return same & (key_pos[None, :] <= query_pos[:, None]) & (key_pos[None, :] >= 0)

def reference(queries, keys, values, grad_out, doc_lengths):
    group = TOK_DEV * N_INNER
    margin = REACH * group
    width = margin + group
    scale = 1.0 / math.sqrt(HEAD_DIM)
    high = lax.Precision.HIGHEST
    key_pad = jnp.concatenate([jnp.zeros((margin, HEAD_DIM), jnp.bfloat16), keys], axis=0)
    val_pad = jnp.concatenate([jnp.zeros((margin, HEAD_DIM), jnp.bfloat16), values], axis=0)
    pos_pad = jnp.concatenate([jnp.full((margin,), -1, jnp.int32), jnp.arange(SEQ, dtype=jnp.int32)])

    def one_group(carry, index):
        dk_acc, dv_acc = carry
        start = (index * group).astype(jnp.int32)
        query_blk = lax.dynamic_slice_in_dim(queries, start, group, 0).reshape(group, HEADS, HEAD_DIM).astype(jnp.float32)
        grad_blk = lax.dynamic_slice_in_dim(grad_out, start, group, 0).reshape(group, HEADS, HEAD_DIM).astype(jnp.float32)
        key_win = lax.dynamic_slice_in_dim(key_pad, start, width, 0).astype(jnp.float32)
        val_win = lax.dynamic_slice_in_dim(val_pad, start, width, 0).astype(jnp.float32)
        key_pos = lax.dynamic_slice_in_dim(pos_pad, start, width, 0)
        query_pos = start + jnp.arange(group, dtype=jnp.int32)
        mask3 = allowed(query_pos, key_pos, doc_lengths)[:, None, :]
        scores = jnp.einsum('thd,kd->thk', query_blk, key_win, precision=high) * scale
        peak = lax.optimization_barrier(jnp.max(jnp.where(mask3, scores, NEG), axis=-1))
        total = lax.optimization_barrier(jnp.sum(jnp.where(mask3, jnp.exp(scores - peak[..., None]), 0.0), axis=-1))
        lse = peak + jnp.log(total)
        probs = jnp.where(mask3, jnp.exp(scores - lse[..., None]), 0.0)
        attended = jnp.einsum('thk,kd->thd', probs, val_win, precision=high)
        delta = lax.optimization_barrier(jnp.sum(grad_blk * attended, axis=-1))
        probs_low = lax.optimization_barrier(probs.astype(jnp.bfloat16)).astype(jnp.float32)
        dv_part = jnp.einsum('thk,thd->kd', probs_low, grad_blk, precision=high)
        dprobs = jnp.einsum('thd,kd->thk', grad_blk, val_win, precision=high)
        dscores = lax.optimization_barrier((probs * (dprobs - delta[..., None])).astype(jnp.bfloat16)).astype(jnp.float32)
        dq_blk = jnp.einsum('thk,kd->thd', dscores, key_win, precision=high) * scale
        dk_part = jnp.einsum('thk,thd->kd', dscores, query_blk, precision=high)
        dk_acc = lax.dynamic_update_slice_in_dim(dk_acc, lax.dynamic_slice_in_dim(dk_acc, start, width, 0) + dk_part, start, 0)
        dv_acc = lax.dynamic_update_slice_in_dim(dv_acc, lax.dynamic_slice_in_dim(dv_acc, start, width, 0) + dv_part, start, 0)
        return ((dk_acc, dv_acc), dq_blk.astype(jnp.bfloat16).reshape(group, HEADS * HEAD_DIM))
    zeros = jnp.zeros((margin + SEQ, HEAD_DIM), jnp.float32)
    (dk_acc, dv_acc), dq_all = lax.scan(one_group, (zeros, zeros), jnp.arange(N_OUTER, dtype=jnp.int32))
    grad_queries = dq_all.reshape(SEQ, HEADS * HEAD_DIM)
    grad_keys = (dk_acc[margin:] * scale).astype(jnp.bfloat16)
    grad_values = dv_acc[margin:].astype(jnp.bfloat16)
    return (grad_queries, grad_keys, grad_values)
```

```python
import functools
import math

import jax
import jax.numpy as jnp
from jax import lax
from jax.experimental import pallas as pl
from jax.experimental.pallas import tpu as pltpu
from jax.sharding import PartitionSpec as P

REACH = 4
NEG = -1e30
AXES = ("outer", "inner")
LANES_CONTRACT = (((1,), (1,)), ((), ()))
ROWS_CONTRACT = (((0,), (0,)), ((), ()))


def permuted(value, target):
    count = lax.axis_size("outer") * lax.axis_size("inner")
    return lax.ppermute(value, AXES, [(at, target(at, count)) for at in range(count)])


def across_core(at, count):
    return at ^ 2


def across_x(at, count):
    return at ^ 1


def ahead(steps, at, count):
    return ((at + steps) % count) ^ ((at >> 1) & 1)


def behind(steps, at, count):
    return ((at ^ ((at >> 1) & 1)) - steps) % count


def own_slots(at):
    turned = at ^ ((at >> 1) & 1)
    slots = [at ^ 1]
    for steps in (8, 4):
        slots += [turned - steps, (turned ^ 2) - steps]
    return slots


def paired_slots(at):
    return [at, at ^ 2] + own_slots(at) + own_slots(at ^ 2)


def grouped_slots(n_inner, at):
    first = at - at % n_inner
    return [first - step * n_inner + j for step in range(REACH + 1) for j in range(n_inner)]


def attention_kernel(slots_of, window, heads, piece_blocks, out_blocks, docs, *refs):
    n_pieces, n_outs = len(piece_blocks), len(out_blocks)
    doc_ref, q_ref, do_ref = refs[:3]
    pieces = refs[3 : 3 + n_pieces]
    dq_ref = refs[3 + n_pieces]
    outs = refs[4 + n_pieces : 4 + n_pieces + n_outs]
    kw, vw, bias, t_buf, dp_buf, dk_acc, dv_acc = refs[4 + n_pieces + n_outs :]
    tokens, head_dim = q_ref.shape[0], kw.shape[1]
    n_inner = lax.axis_size("inner")
    me = lax.axis_index("outer") * n_inner + lax.axis_index("inner")
    slots = slots_of(me)
    scale = 1.0 / math.sqrt(head_dim)

    def rows_of(s):
        return pl.ds(pl.multiple_of(s * tokens, tokens), tokens)

    where = [(ref, i) for ref, n in zip(pieces, piece_blocks) for i in range(n)]
    for slot, (ref, i) in zip(slots, where):
        s = me - slot

        @pl.when((s >= 0) & (s <= window))
        def _():
            kw[rows_of(s), :] = ref[i * tokens : (i + 1) * tokens, :head_dim]
            vw[rows_of(s), :] = ref[i * tokens : (i + 1) * tokens, head_dim:]

    position = me * tokens + lax.broadcasted_iota(jnp.int32, (1, tokens), 1)
    start = jnp.zeros((1, tokens), jnp.int32)
    end = jnp.int32(0)
    for n in range(docs):
        end = end + doc_ref[n]
        start = jnp.where(position >= end, end, start)
    for s in range(window + 1):
        key_at = (me - s) * tokens + lax.broadcasted_iota(jnp.int32, (tokens, tokens), 0)
        seen = (key_at >= start) & (key_at <= position)
        bias[s * tokens : (s + 1) * tokens, :] = jnp.where(seen, 0.0, NEG)

    factor = scale * math.log2(math.e)
    blocks = window + 1

    def one_pair(pair, slot, first):
        def side(ref):
            cut = [
                ref[:, pl.ds(pl.multiple_of((2 * pair + i) * head_dim, head_dim), head_dim)]
                for i in range(2)
            ]
            return jnp.concatenate(cut, axis=0)

        qp, dop = side(q_ref), side(do_ref)
        width = 2 * tokens
        peak = jnp.full((8, width), NEG, jnp.float32)
        for b in range(blocks):
            span = slice(b * tokens, (b + 1) * tokens)
            scores = lax.dot_general(
                kw[span, :], qp, LANES_CONTRACT, preferred_element_type=jnp.float32
            )
            off = bias[span, :]
            t = scores * factor + jnp.concatenate([off, off], axis=1)
            t_buf[slot, span, :] = t
            peak = jnp.maximum(peak, jnp.max(t.reshape(tokens // 8, 8, width), axis=0))
        peak = jnp.max(peak, axis=0, keepdims=True)
        total = jnp.zeros((8, width), jnp.float32)
        moment = jnp.zeros((8, width), jnp.float32)
        for b in range(blocks):
            span = slice(b * tokens, (b + 1) * tokens)
            p = jnp.exp2(t_buf[slot, span, :] - peak)
            dp = lax.dot_general(
                vw[span, :], dop, LANES_CONTRACT, preferred_element_type=jnp.float32
            )
            t_buf[slot, span, :] = p
            dp_buf[slot, span, :] = dp
            total = total + jnp.sum(p.reshape(tokens // 8, 8, width), axis=0)
            moment = moment + jnp.sum((p * dp).reshape(tokens // 8, 8, width), axis=0)
        share = 1.0 / jnp.sum(total, axis=0, keepdims=True)
        delta = jnp.sum(moment, axis=0, keepdims=True) * share
        dq = jnp.zeros((width, head_dim), jnp.float32)
        for b in range(blocks):
            span = slice(b * tokens, (b + 1) * tokens)
            p = t_buf[slot, span, :] * share
            low = p.astype(jnp.bfloat16)
            ds = (p * (dp_buf[slot, span, :] - delta)).astype(jnp.bfloat16)
            dv = jnp.dot(low, dop, preferred_element_type=jnp.float32)
            dk = jnp.dot(ds, qp, preferred_element_type=jnp.float32)
            if first is True:
                dv_acc[span, :] = dv
                dk_acc[span, :] = dk
            else:
                dv_acc[span, :] += dv
                dk_acc[span, :] += dk
            dq = dq + lax.dot_general(
                ds, kw[span, :], ROWS_CONTRACT, preferred_element_type=jnp.float32
            )
        dq = (dq * scale).astype(jnp.bfloat16)
        for i in range(2):
            dq_ref[:, pl.ds(pl.multiple_of((2 * pair + i) * head_dim, head_dim), head_dim)] = dq[
                i * tokens : (i + 1) * tokens
            ]

    n_pairs = heads // 2
    if blocks <= 12:
        for pair in range(n_pairs):
            one_pair(pair, pair % 2, pair == 0)
    else:
        dk_acc[...] = jnp.zeros_like(dk_acc)
        dv_acc[...] = jnp.zeros_like(dv_acc)

        def step(pair, carry):
            one_pair(pair, 0, False)
            return carry

        lax.fori_loop(0, n_pairs, step, 0)

    places = [(ref, i) for ref, n in zip(outs, out_blocks) for i in range(n)]
    for slot, (ref, i) in zip(slots, places):
        s = me - slot
        mine = slice(i * tokens, (i + 1) * tokens)
        inside = (s >= 0) & (s <= window)

        @pl.when(inside)
        def _():
            ref[mine, :head_dim] = dk_acc[rows_of(s), :].astype(ref.dtype)
            ref[mine, head_dim:] = dv_acc[rows_of(s), :].astype(ref.dtype)

        @pl.when(jnp.logical_not(inside))
        def _():
            ref[mine, :] = jnp.zeros((tokens, 2 * head_dim), ref.dtype)


def attend(slots_of, window, queries, grad_out, doc_lengths, pieces, out_blocks, out_types):
    tokens, width = queries.shape
    head_dim = pieces[0].shape[1] // 2
    heads = width // head_dim
    keys = (window + 1) * tokens
    slots = 2 if window + 1 <= 12 else 1
    kernel = functools.partial(
        attention_kernel,
        slots_of,
        window,
        heads,
        [piece.shape[0] // tokens for piece in pieces],
        out_blocks,
        doc_lengths.shape[0],
    )
    whole = pl.BlockSpec(memory_space=pltpu.VMEM)
    return pl.pallas_call(
        kernel,
        out_shape=[jax.ShapeDtypeStruct((tokens, width), jnp.bfloat16)]
        + [
            jax.ShapeDtypeStruct((n * tokens, 2 * head_dim), kind)
            for n, kind in zip(out_blocks, out_types)
        ],
        in_specs=[pl.BlockSpec(memory_space=pltpu.SMEM)] + [whole] * (2 + len(pieces)),
        out_specs=[whole] * (1 + len(out_blocks)),
        scratch_shapes=[
            pltpu.VMEM((keys, head_dim), jnp.bfloat16),
            pltpu.VMEM((keys, head_dim), jnp.bfloat16),
            pltpu.VMEM((keys, tokens), jnp.float32),
            pltpu.VMEM((slots, keys, 2 * tokens), jnp.float32),
            pltpu.VMEM((slots, keys, 2 * tokens), jnp.float32),
            pltpu.VMEM((keys, head_dim), jnp.float32),
            pltpu.VMEM((keys, head_dim), jnp.float32),
        ],
        compiler_params=pltpu.CompilerParams(vmem_limit_bytes=56 * 2**20),
    )(doc_lengths, queries, grad_out, *pieces)


def finish(sums, head_dim):
    scale = 1.0 / math.sqrt(head_dim)
    grad_keys = (sums[:, :head_dim] * scale).astype(jnp.bfloat16)
    return grad_keys, sums[:, head_dim:].astype(jnp.bfloat16)


def paired(queries, keys, values, grad_out, doc_lengths):
    tokens, head_dim = keys.shape
    low, high = jnp.bfloat16, jnp.float32
    own = jnp.concatenate([keys, values], axis=1)
    partner = permuted(own, across_core)
    by_x = permuted(own, across_x)
    both = jnp.concatenate([own, partner], axis=0)
    by_8 = permuted(both, functools.partial(ahead, 8))
    by_4 = permuted(both, functools.partial(ahead, 4))
    fetched = permuted(jnp.concatenate([by_x, by_8, by_4], axis=0), across_core)
    grad_queries, mine, over, keep, give = attend(
        paired_slots,
        REACH * 2,
        queries,
        grad_out,
        doc_lengths,
        [own, partner, by_x, by_8, by_4, fetched],
        [1, 1, 5, 5],
        [high, low, high, low],
    )
    given = permuted(jnp.concatenate([over, give], axis=0), across_core)
    total = (keep + given[tokens:].astype(high)).astype(low)
    back_x = permuted(total[:tokens], across_x)
    back_8 = permuted(total[tokens : 3 * tokens], functools.partial(behind, 8))
    back_4 = permuted(total[3 * tokens :], functools.partial(behind, 4))
    far = back_8.astype(high) + back_4.astype(high)
    last = permuted(far[tokens:].astype(low), across_core)
    sums = (
        mine
        + given[:tokens].astype(high)
        + back_x.astype(high)
        + far[:tokens]
        + last.astype(high)
    )
    return (grad_queries,) + finish(sums, head_dim)


def grouped(queries, keys, values, grad_out, doc_lengths):
    tokens, head_dim = keys.shape
    n_inner, n_outer = lax.axis_size("inner"), lax.axis_size("outer")

    def turned(value, steps):
        return lax.ppermute(
            value, "outer", [(at, (at + steps) % n_outer) for at in range(n_outer)]
        )

    own = jnp.concatenate([keys, values], axis=1)
    group = lax.all_gather(own, "inner", axis=0, tiled=True)
    pieces = [group] + [turned(group, step) for step in range(1, REACH + 1)]
    results = attend(
        functools.partial(grouped_slots, n_inner),
        REACH * n_inner,
        queries,
        grad_out,
        doc_lengths,
        pieces,
        [n_inner] * (REACH + 1),
        [jnp.float32] * (REACH + 1),
    )
    sums = results[1]
    for step in range(1, REACH + 1):
        sums = sums + turned(results[1 + step], -step)
    sums = lax.psum_scatter(sums, "inner", scatter_dimension=0, tiled=True)
    return (results[0],) + finish(sums, head_dim)


def on_device(queries, keys, values, grad_out, doc_lengths):
    if lax.axis_size("inner") == 2 and lax.axis_size("outer") % 4 == 0:
        return paired(queries, keys, values, grad_out, doc_lengths)
    return grouped(queries, keys, values, grad_out, doc_lengths)


def solution(mesh):
    rows = P(("outer", "inner"), None)
    return jax.shard_map(
        on_device,
        mesh=mesh,
        in_specs=(rows, rows, rows, rows, P()),
        out_specs=(rows, rows, rows),
        check_vma=False,
    )
```

```python
import functools
import math

import jax
import jax.numpy as jnp
from jax import lax
from jax.experimental import pallas as pl
from jax.experimental.pallas import tpu as pltpu
from jax.sharding import PartitionSpec as P

REACH = 4
NEG = -1e30
AXES = ("outer", "inner")
LANES_CONTRACT = (((1,), (1,)), ((), ()))
ROWS_CONTRACT = (((0,), (0,)), ((), ()))


def permuted(value, target):
    count = lax.axis_size("outer") * lax.axis_size("inner")
    return lax.ppermute(value, AXES, [(at, target(at, count)) for at in range(count)])


def across_core(at, count):
    return at ^ 2


def across_x(at, count):
    return at ^ 1


def ahead(steps, at, count):
    return ((at + steps) % count) ^ ((at >> 1) & 1)


def behind(steps, at, count):
    return ((at ^ ((at >> 1) & 1)) - steps) % count


def own_slots(at):
    turned = at ^ ((at >> 1) & 1)
    slots = [at ^ 1]
    for steps in (8, 4):
        slots += [turned - steps, (turned ^ 2) - steps]
    return slots


def paired_slots(at):
    return [at, at ^ 2] + own_slots(at) + own_slots(at ^ 2)


def paired_given(at):
    return [at] + own_slots(at) + [at ^ 2] + own_slots(at ^ 2)


def grouped_slots(n_inner, at):
    first = at - at % n_inner
    return [first - step * n_inner + j for step in range(REACH + 1) for j in range(n_inner)]


def attention_kernel(slots_of, given_of, window, heads, piece_blocks, out_blocks, docs, *refs):
    n_pieces, n_outs = len(piece_blocks), len(out_blocks)
    doc_ref, q_ref, do_ref = refs[:3]
    pieces = refs[3 : 3 + n_pieces]
    dq_ref = refs[3 + n_pieces]
    outs = refs[4 + n_pieces : 4 + n_pieces + n_outs]
    kw, vw, bias, t_buf, dp_buf, dk_acc, dv_acc = refs[4 + n_pieces + n_outs :]
    tokens, head_dim = q_ref.shape[0], kw.shape[1]
    n_inner = lax.axis_size("inner")
    me = lax.axis_index("outer") * n_inner + lax.axis_index("inner")
    slots = slots_of(me)
    scale = 1.0 / math.sqrt(head_dim)

    def rows_of(s):
        return pl.ds(pl.multiple_of(s * tokens, tokens), tokens)

    where = [(ref, i) for ref, n in zip(pieces, piece_blocks) for i in range(n)]
    for slot, (ref, i) in zip(slots, where):
        s = me - slot

        @pl.when((s >= 0) & (s <= window))
        def _():
            kw[rows_of(s), :] = ref[2 * i * tokens : (2 * i + 1) * tokens, :]
            vw[rows_of(s), :] = ref[(2 * i + 1) * tokens : (2 * i + 2) * tokens, :]

    position = me * tokens + lax.broadcasted_iota(jnp.int32, (1, tokens), 1)
    start = jnp.zeros((1, tokens), jnp.int32)
    end = jnp.int32(0)
    for n in range(docs):
        end = end + doc_ref[n]
        start = jnp.where(position >= end, end, start)
    for s in range(window + 1):
        key_at = (me - s) * tokens + lax.broadcasted_iota(jnp.int32, (tokens, tokens), 0)
        seen = (key_at >= start) & (key_at <= position)
        bias[s * tokens : (s + 1) * tokens, :] = jnp.where(seen, 0.0, NEG)

    factor = scale * math.log2(math.e)
    blocks = window + 1

    def one_pair(pair, slot, first):
        def side(ref):
            cut = [
                ref[:, pl.ds(pl.multiple_of((2 * pair + i) * head_dim, head_dim), head_dim)]
                for i in range(2)
            ]
            return jnp.concatenate(cut, axis=0)

        qp, dop = side(q_ref), side(do_ref)
        width = 2 * tokens
        peak = jnp.full((8, width), NEG, jnp.float32)
        for b in range(blocks):
            span = slice(b * tokens, (b + 1) * tokens)
            scores = lax.dot_general(
                kw[span, :], qp, LANES_CONTRACT, preferred_element_type=jnp.float32
            )
            off = bias[span, :]
            t = scores * factor + jnp.concatenate([off, off], axis=1)
            t_buf[slot, span, :] = t
            peak = jnp.maximum(peak, jnp.max(t.reshape(tokens // 8, 8, width), axis=0))
        peak = jnp.max(peak, axis=0, keepdims=True)
        total = jnp.zeros((8, width), jnp.float32)
        moment = jnp.zeros((8, width), jnp.float32)
        for b in range(blocks):
            span = slice(b * tokens, (b + 1) * tokens)
            p = jnp.exp2(t_buf[slot, span, :] - peak)
            dp = lax.dot_general(
                vw[span, :], dop, LANES_CONTRACT, preferred_element_type=jnp.float32
            )
            t_buf[slot, span, :] = p
            dp_buf[slot, span, :] = dp
            total = total + jnp.sum(p.reshape(tokens // 8, 8, width), axis=0)
            moment = moment + jnp.sum((p * dp).reshape(tokens // 8, 8, width), axis=0)
        share = 1.0 / jnp.sum(total, axis=0, keepdims=True)
        delta = jnp.sum(moment, axis=0, keepdims=True) * share
        dq = jnp.zeros((width, head_dim), jnp.float32)
        for b in range(blocks):
            span = slice(b * tokens, (b + 1) * tokens)
            p = t_buf[slot, span, :] * share
            low = p.astype(jnp.bfloat16)
            ds = (p * (dp_buf[slot, span, :] - delta)).astype(jnp.bfloat16)
            dv = jnp.dot(low, dop, preferred_element_type=jnp.float32)
            dk = jnp.dot(ds, qp, preferred_element_type=jnp.float32)
            if first is True:
                dv_acc[span, :] = dv
                dk_acc[span, :] = dk
            else:
                dv_acc[span, :] += dv
                dk_acc[span, :] += dk
            dq = dq + lax.dot_general(
                ds, kw[span, :], ROWS_CONTRACT, preferred_element_type=jnp.float32
            )
        dq = (dq * scale).astype(jnp.bfloat16)
        for i in range(2):
            dq_ref[:, pl.ds(pl.multiple_of((2 * pair + i) * head_dim, head_dim), head_dim)] = dq[
                i * tokens : (i + 1) * tokens
            ]

    n_pairs = heads // 2
    if blocks <= 12:
        for pair in range(n_pairs):
            one_pair(pair, pair % 2, pair == 0)
    else:
        dk_acc[...] = jnp.zeros_like(dk_acc)
        dv_acc[...] = jnp.zeros_like(dv_acc)

        def step(pair, carry):
            one_pair(pair, 0, False)
            return carry

        lax.fori_loop(0, n_pairs, step, 0)

    places = [(ref, i) for ref, n in zip(outs, out_blocks) for i in range(n)]
    for slot, (ref, i) in zip(given_of(me), places):
        s = me - slot
        first, second = (slice((2 * i + j) * tokens, (2 * i + j + 1) * tokens) for j in range(2))
        inside = (s >= 0) & (s <= window)

        @pl.when(inside)
        def _():
            ref[first, :] = dk_acc[rows_of(s), :].astype(ref.dtype)
            ref[second, :] = dv_acc[rows_of(s), :].astype(ref.dtype)

        @pl.when(jnp.logical_not(inside))
        def _():
            ref[first, :] = jnp.zeros((tokens, head_dim), ref.dtype)
            ref[second, :] = jnp.zeros((tokens, head_dim), ref.dtype)


def attend(slots_of, given_of, window, queries, grad_out, doc_lengths, pieces, out_blocks, out_types):
    tokens, width = queries.shape
    head_dim = pieces[0].shape[1]
    heads = width // head_dim
    keys = (window + 1) * tokens
    slots = 2 if window + 1 <= 12 else 1
    kernel = functools.partial(
        attention_kernel,
        slots_of,
        given_of,
        window,
        heads,
        [piece.shape[0] // (2 * tokens) for piece in pieces],
        out_blocks,
        doc_lengths.shape[0],
    )
    whole = pl.BlockSpec(memory_space=pltpu.VMEM)
    return pl.pallas_call(
        kernel,
        out_shape=[jax.ShapeDtypeStruct((tokens, width), jnp.bfloat16)]
        + [
            jax.ShapeDtypeStruct((2 * n * tokens, head_dim), kind)
            for n, kind in zip(out_blocks, out_types)
        ],
        in_specs=[pl.BlockSpec(memory_space=pltpu.SMEM)] + [whole] * (2 + len(pieces)),
        out_specs=[whole] * (1 + len(out_blocks)),
        scratch_shapes=[
            pltpu.VMEM((keys, head_dim), jnp.bfloat16),
            pltpu.VMEM((keys, head_dim), jnp.bfloat16),
            pltpu.VMEM((keys, tokens), jnp.float32),
            pltpu.VMEM((slots, keys, 2 * tokens), jnp.float32),
            pltpu.VMEM((slots, keys, 2 * tokens), jnp.float32),
            pltpu.VMEM((keys, head_dim), jnp.float32),
            pltpu.VMEM((keys, head_dim), jnp.float32),
        ],
        compiler_params=pltpu.CompilerParams(vmem_limit_bytes=(16 if window <= 12 else 56) * 2**20),
    )(doc_lengths, queries, grad_out, *pieces)


def finish(sums, head_dim):
    scale = 1.0 / math.sqrt(head_dim)
    half = sums.shape[0] // 2
    grad_keys = (sums[:half] * scale).astype(jnp.bfloat16)
    return grad_keys, sums[half:].astype(jnp.bfloat16)


def paired(queries, keys, values, grad_out, doc_lengths):
    tokens, head_dim = keys.shape
    low, high = jnp.bfloat16, jnp.float32
    block = 2 * tokens
    own = jnp.concatenate([keys, values], axis=0)
    partner = permuted(own, across_core)
    by_x = permuted(own, across_x)
    both = jnp.concatenate([own, partner], axis=0)
    by_4 = permuted(both, functools.partial(ahead, 4))
    by_8 = permuted(both, functools.partial(ahead, 8))
    fetched = permuted(jnp.concatenate([by_x, by_8, by_4], axis=0), across_core)
    grad_queries, mine, keep, give = attend(
        paired_slots,
        paired_given,
        REACH * 2,
        queries,
        grad_out,
        doc_lengths,
        [own, partner, by_x, by_8, by_4, fetched],
        [1, 5, 6],
        [high, high, low],
    )
    given = permuted(give, across_core)
    total = (keep + given[block:].astype(high)).astype(low)
    back_4 = permuted(total[3 * block :], functools.partial(behind, 4))
    back_8 = permuted(total[block : 3 * block], functools.partial(behind, 8))
    back_x = permuted(total[:block], across_x)
    far = back_8.astype(high) + back_4.astype(high)
    last = permuted(far[block:].astype(low), across_core)
    sums = (
        mine
        + given[:block].astype(high)
        + back_x.astype(high)
        + far[:block]
        + last.astype(high)
    )
    return (grad_queries,) + finish(sums, head_dim)


def grouped(queries, keys, values, grad_out, doc_lengths):
    tokens, head_dim = keys.shape
    n_inner, n_outer = lax.axis_size("inner"), lax.axis_size("outer")

    def turned(value, steps):
        return lax.ppermute(
            value, "outer", [(at, (at + steps) % n_outer) for at in range(n_outer)]
        )

    own = jnp.concatenate([keys, values], axis=0)
    group = lax.all_gather(own, "inner", axis=0, tiled=True)
    pieces = [group] + [turned(group, step) for step in range(1, REACH + 1)]
    results = attend(
        functools.partial(grouped_slots, n_inner),
        functools.partial(grouped_slots, n_inner),
        REACH * n_inner,
        queries,
        grad_out,
        doc_lengths,
        pieces,
        [n_inner] * (REACH + 1),
        [jnp.float32] * (REACH + 1),
    )
    sums = results[1]
    for step in range(1, REACH + 1):
        sums = sums + turned(results[1 + step], -step)
    sums = lax.psum_scatter(sums, "inner", scatter_dimension=0, tiled=True)
    return (results[0],) + finish(sums, head_dim)


def on_device(queries, keys, values, grad_out, doc_lengths):
    if lax.axis_size("inner") == 2 and lax.axis_size("outer") % 4 == 0:
        return paired(queries, keys, values, grad_out, doc_lengths)
    return grouped(queries, keys, values, grad_out, doc_lengths)


def solution(mesh):
    rows = P(("outer", "inner"), None)
    return jax.shard_map(
        on_device,
        mesh=mesh,
        in_specs=(rows, rows, rows, rows, P()),
        out_specs=(rows, rows, rows),
        check_vma=False,
    )
```

```python
import functools
import math

import jax
import jax.numpy as jnp
from jax import lax
from jax.experimental import pallas as pl
from jax.experimental.pallas import tpu as pltpu
from jax.sharding import PartitionSpec as P

REACH = 4
NEG = -1e30
AXES = ("outer", "inner")
LANES_CONTRACT = (((1,), (1,)), ((), ()))
ROWS_CONTRACT = (((0,), (0,)), ((), ()))


def permuted(value, target):
    count = lax.axis_size("outer") * lax.axis_size("inner")
    return lax.ppermute(value, AXES, [(at, target(at, count)) for at in range(count)])


def across_core(at, count):
    return at ^ 2


def across_x(at, count):
    return at ^ 1


def ahead(steps, at, count):
    return ((at + steps) % count) ^ ((at >> 1) & 1)


def behind(steps, at, count):
    return ((at ^ ((at >> 1) & 1)) - steps) % count


def own_slots(at):
    turned = at ^ ((at >> 1) & 1)
    slots = [at ^ 1]
    for steps in (8, 4):
        slots += [turned - steps, (turned ^ 2) - steps]
    return slots


def grouped_slots(n_inner, at):
    first = at - at % n_inner
    return [first - step * n_inner + j for step in range(REACH + 1) for j in range(n_inner)]


def attention_kernel(slots_of, given_of, window, heads, piece_blocks, out_blocks, docs, *refs):
    n_pieces, n_outs = len(piece_blocks), len(out_blocks)
    doc_ref, q_ref, do_ref = refs[:3]
    pieces = refs[3 : 3 + n_pieces]
    dq_ref = refs[3 + n_pieces]
    outs = refs[4 + n_pieces : 4 + n_pieces + n_outs]
    kw, vw, bias, t_buf, dp_buf, dk_acc, dv_acc = refs[4 + n_pieces + n_outs :]
    tokens, head_dim = q_ref.shape[0], kw.shape[1]
    n_inner = lax.axis_size("inner")
    me = lax.axis_index("outer") * n_inner + lax.axis_index("inner")
    slots = slots_of(me)
    scale = 1.0 / math.sqrt(head_dim)

    def rows_of(s):
        return pl.ds(pl.multiple_of(s * tokens, tokens), tokens)

    where = [(ref, i) for ref, n in zip(pieces, piece_blocks) for i in range(n)]
    for slot, (ref, i) in zip(slots, where):
        s = me - slot

        @pl.when((s >= 0) & (s <= window))
        def _():
            kw[rows_of(s), :] = ref[2 * i * tokens : (2 * i + 1) * tokens, :]
            vw[rows_of(s), :] = ref[(2 * i + 1) * tokens : (2 * i + 2) * tokens, :]

    position = me * tokens + lax.broadcasted_iota(jnp.int32, (1, tokens), 1)
    start = jnp.zeros((1, tokens), jnp.int32)
    end = jnp.int32(0)
    for n in range(docs):
        end = end + doc_ref[n]
        start = jnp.where(position >= end, end, start)
    for s in range(window + 1):
        key_at = (me - s) * tokens + lax.broadcasted_iota(jnp.int32, (tokens, tokens), 0)
        seen = (key_at >= start) & (key_at <= position)
        bias[s * tokens : (s + 1) * tokens, :] = jnp.where(seen, 0.0, NEG)

    factor = scale * math.log2(math.e)
    blocks = window + 1

    def one_pair(pair, slot, first):
        def side(ref):
            cut = [
                ref[:, pl.ds(pl.multiple_of((2 * pair + i) * head_dim, head_dim), head_dim)]
                for i in range(2)
            ]
            return jnp.concatenate(cut, axis=0)

        qp, dop = side(q_ref), side(do_ref)
        width = 2 * tokens
        peak = jnp.full((8, width), NEG, jnp.float32)
        for b in range(blocks):
            span = slice(b * tokens, (b + 1) * tokens)
            scores = lax.dot_general(
                kw[span, :], qp, LANES_CONTRACT, preferred_element_type=jnp.float32
            )
            off = bias[span, :]
            t = scores * factor + jnp.concatenate([off, off], axis=1)
            t_buf[slot, span, :] = t
            peak = jnp.maximum(peak, jnp.max(t.reshape(tokens // 8, 8, width), axis=0))
        peak = jnp.max(peak, axis=0, keepdims=True)
        total = jnp.zeros((8, width), jnp.float32)
        moment = jnp.zeros((8, width), jnp.float32)
        for b in range(blocks):
            span = slice(b * tokens, (b + 1) * tokens)
            p = jnp.exp2(t_buf[slot, span, :] - peak)
            dp = lax.dot_general(
                vw[span, :], dop, LANES_CONTRACT, preferred_element_type=jnp.float32
            )
            t_buf[slot, span, :] = p
            dp_buf[slot, span, :] = dp
            total = total + jnp.sum(p.reshape(tokens // 8, 8, width), axis=0)
            moment = moment + jnp.sum((p * dp).reshape(tokens // 8, 8, width), axis=0)
        share = 1.0 / jnp.sum(total, axis=0, keepdims=True)
        delta = jnp.sum(moment, axis=0, keepdims=True) * share
        dq = jnp.zeros((width, head_dim), jnp.float32)
        for b in range(blocks):
            span = slice(b * tokens, (b + 1) * tokens)
            p = t_buf[slot, span, :] * share
            low = p.astype(jnp.bfloat16)
            ds = (p * (dp_buf[slot, span, :] - delta)).astype(jnp.bfloat16)
            dv = jnp.dot(low, dop, preferred_element_type=jnp.float32)
            dk = jnp.dot(ds, qp, preferred_element_type=jnp.float32)
            if first is True:
                dv_acc[span, :] = dv
                dk_acc[span, :] = dk
            else:
                dv_acc[span, :] += dv
                dk_acc[span, :] += dk
            dq = dq + lax.dot_general(
                ds, kw[span, :], ROWS_CONTRACT, preferred_element_type=jnp.float32
            )
        dq = (dq * scale).astype(jnp.bfloat16)
        for i in range(2):
            dq_ref[:, pl.ds(pl.multiple_of((2 * pair + i) * head_dim, head_dim), head_dim)] = dq[
                i * tokens : (i + 1) * tokens
            ]

    n_pairs = heads // 2
    if blocks <= 12:
        for pair in range(n_pairs):
            one_pair(pair, pair % 2, pair == 0)
    else:
        dk_acc[...] = jnp.zeros_like(dk_acc)
        dv_acc[...] = jnp.zeros_like(dv_acc)

        def step(pair, carry):
            one_pair(pair, 0, False)
            return carry

        lax.fori_loop(0, n_pairs, step, 0)

    places = [(ref, i) for ref, n in zip(outs, out_blocks) for i in range(n)]
    for slot, (ref, i) in zip(given_of(me), places):
        s = me - slot
        first, second = (slice((2 * i + j) * tokens, (2 * i + j + 1) * tokens) for j in range(2))
        inside = (s >= 0) & (s <= window)

        @pl.when(inside)
        def _():
            ref[first, :] = dk_acc[rows_of(s), :].astype(ref.dtype)
            ref[second, :] = dv_acc[rows_of(s), :].astype(ref.dtype)

        @pl.when(jnp.logical_not(inside))
        def _():
            ref[first, :] = jnp.zeros((tokens, head_dim), ref.dtype)
            ref[second, :] = jnp.zeros((tokens, head_dim), ref.dtype)


def attend(slots_of, given_of, window, queries, grad_out, doc_lengths, pieces, out_blocks, out_types):
    tokens, width = queries.shape
    head_dim = pieces[0].shape[1]
    heads = width // head_dim
    keys = (window + 1) * tokens
    slots = 2 if window + 1 <= 12 else 1
    kernel = functools.partial(
        attention_kernel,
        slots_of,
        given_of,
        window,
        heads,
        [piece.shape[0] // (2 * tokens) for piece in pieces],
        out_blocks,
        doc_lengths.shape[0],
    )
    whole = pl.BlockSpec(memory_space=pltpu.VMEM)
    return pl.pallas_call(
        kernel,
        out_shape=[jax.ShapeDtypeStruct((tokens, width), jnp.bfloat16)]
        + [
            jax.ShapeDtypeStruct((2 * n * tokens, head_dim), kind)
            for n, kind in zip(out_blocks, out_types)
        ],
        in_specs=[pl.BlockSpec(memory_space=pltpu.SMEM)] + [whole] * (2 + len(pieces)),
        out_specs=[whole] * (1 + len(out_blocks)),
        scratch_shapes=[
            pltpu.VMEM((keys, head_dim), jnp.bfloat16),
            pltpu.VMEM((keys, head_dim), jnp.bfloat16),
            pltpu.VMEM((keys, tokens), jnp.float32),
            pltpu.VMEM((slots, keys, 2 * tokens), jnp.float32),
            pltpu.VMEM((slots, keys, 2 * tokens), jnp.float32),
            pltpu.VMEM((keys, head_dim), jnp.float32),
            pltpu.VMEM((keys, head_dim), jnp.float32),
        ],
        compiler_params=pltpu.CompilerParams(vmem_limit_bytes=(16 if window <= 12 else 56) * 2**20),
    )(doc_lengths, queries, grad_out, *pieces)


def finish(sums, head_dim):
    scale = 1.0 / math.sqrt(head_dim)
    half = sums.shape[0] // 2
    grad_keys = (sums[:half] * scale).astype(jnp.bfloat16)
    return grad_keys, sums[half:].astype(jnp.bfloat16)


def head_rows(ref, rows):
    tokens = ref.shape[0]
    head_dim = rows.shape[1]
    for h in range(rows.shape[0] // tokens):
        rows[h * tokens : (h + 1) * tokens, :] = ref[:, h * head_dim : (h + 1) * head_dim]


def own_position():
    return lax.axis_index("outer") * lax.axis_size("inner") + lax.axis_index("inner")


def document_starts(doc_ref, docs, position):
    start = jnp.zeros(position.shape, jnp.int32)
    end = jnp.int32(0)
    for n in range(docs):
        end = end + doc_ref[n]
        start = jnp.where(position >= end, end, start)
    return start


def score_blocks(ids, blocks, start, me, q_rows, do_rows, bias, p_ref, dp_ref):
    rows, head_dim = q_rows.shape
    tokens = bias.shape[1]
    factor = math.log2(math.e) / math.sqrt(head_dim)
    position = me * tokens + lax.broadcasted_iota(jnp.int32, (1, tokens), 1)
    spans = [slice(b * tokens, (b + 1) * tokens) for b in range(len(blocks))]
    for span, at in zip(spans, ids):
        key_at = at * tokens + lax.broadcasted_iota(jnp.int32, (tokens, tokens), 0)
        seen = (key_at >= start) & (key_at <= position)
        bias[span, :] = jnp.where(seen, 0.0, NEG)
    width = 2 * tokens
    stats = []
    for pair in range(rows // width):
        cols = slice(pair * width, (pair + 1) * width)
        qp, dop = q_rows[cols, :], do_rows[cols, :]
        peak = jnp.full((8, width), NEG, jnp.float32)
        for span, (keys, values) in zip(spans, blocks):
            scores = lax.dot_general(
                keys(), qp, LANES_CONTRACT, preferred_element_type=jnp.float32
            )
            off = bias[span, :]
            t = scores * factor + jnp.concatenate([off, off], axis=1)
            p_ref[span, cols] = t
            peak = jnp.maximum(peak, jnp.max(t.reshape(tokens // 8, 8, width), axis=0))
        peak = jnp.max(peak, axis=0, keepdims=True)
        total = jnp.zeros((8, width), jnp.float32)
        moment = jnp.zeros((8, width), jnp.float32)
        for span, (keys, values) in zip(spans, blocks):
            p = jnp.exp2(p_ref[span, cols] - peak)
            dp = lax.dot_general(
                values(), dop, LANES_CONTRACT, preferred_element_type=jnp.float32
            )
            p_ref[span, cols] = p
            dp_ref[span, cols] = dp
            total = total + jnp.sum(p.reshape(tokens // 8, 8, width), axis=0)
            moment = moment + jnp.sum((p * dp).reshape(tokens // 8, 8, width), axis=0)
        stats.append(
            (
                peak,
                jnp.sum(total, axis=0, keepdims=True),
                jnp.sum(moment, axis=0, keepdims=True),
            )
        )
    return [jnp.concatenate(parts, axis=1) for parts in zip(*stats)]


def grad_block(p_ref, dp_ref, span, share, delta, q_rows, do_rows, ds_ref, ds_span):
    p = p_ref[span, :] * share
    low = p.astype(jnp.bfloat16)
    ds = (p * (dp_ref[span, :] - delta)).astype(jnp.bfloat16)
    ds_ref[ds_span, :] = ds
    dk = jnp.dot(ds, q_rows[...], preferred_element_type=jnp.float32)
    dv = jnp.dot(low, do_rows[...], preferred_element_type=jnp.float32)
    return dk, dv


def block_of(ref, i, tokens):
    return (
        lambda: ref[2 * i * tokens : (2 * i + 1) * tokens, :],
        lambda: ref[(2 * i + 1) * tokens : (2 * i + 2) * tokens, :],
    )


def put_block(ref, i, dk, dv):
    tokens = dk.shape[0]
    ref[2 * i * tokens : (2 * i + 1) * tokens, :] = dk.astype(ref.dtype)
    ref[(2 * i + 1) * tokens : (2 * i + 2) * tokens, :] = dv.astype(ref.dtype)


def pack_kernel(keys, values, own, sems):
    tokens = keys.shape[0]
    copies = [
        pltpu.make_async_copy(ref, own.at[pl.ds(i * tokens, tokens), :], sems.at[i])
        for i, ref in enumerate((keys, values))
    ]
    for copy in copies:
        copy.start()
    for copy in copies:
        copy.wait()


def near_kernel(
    docs, doc_hbm, q_hbm, do_hbm, own, partner,
    p_out, dp_out, stats, q_rows, do_rows, starts,
    bias, doc_ref, sems,
):
    me = own_position()
    tokens = q_hbm.shape[0]
    rows, head_dim = q_rows.shape
    heads = rows // tokens
    copies = [pltpu.make_async_copy(doc_hbm, doc_ref, sems.at[2 * heads])]
    for i, (source, stacked) in enumerate(((q_hbm, q_rows), (do_hbm, do_rows))):
        for h in range(heads):
            copies.append(
                pltpu.make_async_copy(
                    source.at[:, pl.ds(h * head_dim, head_dim)],
                    stacked.at[pl.ds(h * tokens, tokens), :],
                    sems.at[i * heads + h],
                )
            )
    for copy in copies:
        copy.start()
    for copy in copies:
        copy.wait()
    position = me * tokens + lax.broadcasted_iota(jnp.int32, (1, tokens), 1)
    start = document_starts(doc_ref, docs, position)
    starts[0:1, :] = start
    peak, total, moment = score_blocks(
        [me, me ^ 2],
        [block_of(own, 0, tokens), block_of(partner, 0, tokens)],
        start, me, q_rows, do_rows, bias, p_out, dp_out,
    )
    stats[0:1, :], stats[1:2, :], stats[2:3, :] = peak, total, moment


def direct_kernel(q_rows, do_rows, starts, by_x, by_8, by_4, p_out, dp_out, stats, bias):
    me = own_position()
    tokens = starts.shape[1]
    peak, total, moment = score_blocks(
        own_slots(me),
        [block_of(by_x, 0, tokens)] + [block_of(ref, i, tokens) for ref in (by_8, by_4) for i in range(2)],
        starts[0:1, :], me, q_rows, do_rows, bias, p_out, dp_out,
    )
    stats[0:1, :], stats[1:2, :], stats[2:3, :] = peak, total, moment


def fetched_ids(me):
    slots = own_slots(me ^ 2)
    return [jnp.where((me >> 1) & 1 == 0, slots[1], slots[0])] + slots[2:]


def fetched_kernel(
    q_rows, do_rows, starts, fetched, p_near, dp_near, stats_near, stats_direct,
    give, ds_out, shares, bias, p_buf, dp_buf,
):
    me = own_position()
    tokens = starts.shape[1]
    ids = fetched_ids(me)
    peak, total, moment = score_blocks(
        ids,
        [block_of(fetched, i, tokens) for i in range(4)],
        starts[0:1, :], me, q_rows, do_rows, bias, p_buf, dp_buf,
    )
    parts = [(ref[0:1, :], ref[1:2, :], ref[2:3, :]) for ref in (stats_near, stats_direct)]
    parts.append((peak, total, moment))
    top = jnp.maximum(jnp.maximum(parts[0][0], parts[1][0]), peak)
    factors = [jnp.exp2(part[0] - top) for part in parts]
    one = 1.0 / sum(f * part[1] for f, part in zip(factors, parts))
    delta = sum(f * part[2] for f, part in zip(factors, parts)) * one
    shared = [f * one for f in factors]
    shares[0:1, :], shares[1:2, :], shares[2:3, :] = shared[0], shared[1], delta
    for i in range(4):
        span = slice(i * tokens, (i + 1) * tokens)
        put_block(give, 1 + i, *grad_block(p_buf, dp_buf, span, shared[2], delta, q_rows, do_rows, ds_out, span))
    put_block(
        give, 0,
        *grad_block(
            p_near, dp_near, slice(tokens, 2 * tokens), shared[0], delta, q_rows, do_rows,
            ds_out, slice(4 * tokens, 5 * tokens),
        ),
    )


def keep_kernel(q_rows, do_rows, p_ref, dp_ref, shares, keep, ds_out):
    tokens = p_ref.shape[0] // 5
    share, delta = shares[1:2, :], shares[2:3, :]
    for i in range(5):
        span = slice(i * tokens, (i + 1) * tokens)
        put_block(keep, i, *grad_block(p_ref, dp_ref, span, share, delta, q_rows, do_rows, ds_out, span))


def query_kernel(
    q_rows, do_rows, p_ref, dp_ref, shares, ds_fetched, ds_direct, fetched, partner, by_x, by_8, by_4, own,
    dq_ref, mine, ds_own,
):
    tokens = dq_ref.shape[0]
    head_dim = own.shape[1]
    scale = 1.0 / math.sqrt(head_dim)
    span = slice(0, tokens)
    put_block(
        mine, 0, *grad_block(p_ref, dp_ref, span, shares[0:1, :], shares[2:3, :], q_rows, do_rows, ds_own, span)
    )
    where = [(ds_fetched, i, block_of(fetched, i, tokens)) for i in range(4)]
    where.append((ds_fetched, 4, block_of(partner, 0, tokens)))
    direct = [(by_x, 0)] + [(ref, i) for ref in (by_8, by_4) for i in range(2)]
    where += [(ds_direct, n, block_of(ref, i, tokens)) for n, (ref, i) in enumerate(direct)]
    where.append((ds_own, 0, block_of(own, 0, tokens)))
    width = 2 * tokens
    for pair in range(q_rows.shape[0] // width):
        cols = slice(pair * width, (pair + 1) * width)
        dq = jnp.zeros((width, head_dim), jnp.float32)
        for ref, n, (keys, values) in where:
            dq = dq + lax.dot_general(
                ref[n * tokens : (n + 1) * tokens, cols], keys(), ROWS_CONTRACT,
                preferred_element_type=jnp.float32,
            )
        dq = (dq * scale).astype(jnp.bfloat16)
        for i in range(2):
            h = 2 * pair + i
            dq_ref[:, h * head_dim : (h + 1) * head_dim] = dq[i * tokens : (i + 1) * tokens]


def result_kernel(mine, given, back_x, far, last, dk_ref, dv_ref):
    tokens, head_dim = dk_ref.shape
    high = jnp.float32
    for half, (ref, scale) in enumerate(((dk_ref, 1.0 / math.sqrt(head_dim)), (dv_ref, 1.0))):
        span = slice(half * tokens, (half + 1) * tokens)
        sums = mine[span, :] + given[span, :].astype(high) + back_x[span, :].astype(high)
        sums = sums + far[span, :] + last[span, :].astype(high)
        ref[...] = (sums * scale).astype(ref.dtype)


def local_call(kernel, outs, scratch, args, blocks, far=0):
    whole = pl.BlockSpec(memory_space=pltpu.VMEM)
    specs = [pl.BlockSpec(memory_space=pltpu.HBM)] * far + [whole] * (len(args) - far)
    return pl.pallas_call(
        kernel,
        out_shape=[jax.ShapeDtypeStruct(shape, kind) for shape, kind in outs],
        in_specs=specs,
        out_specs=[whole] * len(outs),
        scratch_shapes=[
            pltpu.VMEM(*entry) if isinstance(entry, tuple) else entry for entry in scratch
        ],
        compiler_params=pltpu.CompilerParams(vmem_limit_bytes=16 * 2**20),
        cost_estimate=pl.CostEstimate(
            flops=blocks * 2 * 128 * 128 * 1024, bytes_accessed=blocks * 2**19, transcendentals=0
        ),
    )(*[pltpu.with_memory_space_constraint(arg, pltpu.HBM) for arg in args[:far]], *args[far:])


def paired(queries, keys, values, grad_out, doc_lengths):
    tokens, head_dim = keys.shape
    low, high = jnp.bfloat16, jnp.float32
    block = 2 * tokens
    rows = queries.shape[1] // head_dim * tokens
    docs = doc_lengths.shape[0]
    second = (own_position() >> 1) & 1

    def part(n):
        return [((n * tokens, rows), high)] * 2 + [((8, rows), high)], [((n * tokens, tokens), high)]

    (own,) = local_call(
        pack_kernel, [((block, head_dim), low)], [pltpu.SemaphoreType.DMA((2,))], [keys, values], 0, far=2
    )
    partner = permuted(own, across_core)
    by_x = permuted(own, across_x)
    both = jnp.concatenate([own, partner], axis=0)
    by_4 = permuted(both, functools.partial(ahead, 4))
    by_8 = permuted(both, functools.partial(ahead, 8))
    outs, scratch = part(2)
    p_near, dp_near, stats_near, q_rows, do_rows, starts = local_call(
        functools.partial(near_kernel, docs),
        outs + [((rows, head_dim), low)] * 2 + [((8, tokens), jnp.int32)],
        scratch
        + [
            pltpu.SMEM(doc_lengths.shape, jnp.int32),
            pltpu.SemaphoreType.DMA((2 * (rows // tokens) + 1,)),
        ],
        [doc_lengths, queries, grad_out, own, partner],
        4,
        far=3,
    )
    by_x, by_8, by_4, stats_near = lax.optimization_barrier((by_x, by_8, by_4, stats_near))
    offered = jnp.where(second == 0, by_x, by_8[:block])
    fetched = permuted(jnp.concatenate([offered, by_8[block:], by_4], axis=0), across_core)
    p_direct, dp_direct, stats_direct = local_call(
        direct_kernel, *part(5), [q_rows, do_rows, starts, by_x, by_8, by_4], 10
    )
    give, ds_fetched, shares = local_call(
        fetched_kernel,
        [((5 * block, head_dim), low), ((5 * tokens, rows), low), ((8, rows), high)],
        part(4)[1] + [((4 * tokens, rows), high)] * 2,
        [q_rows, do_rows, starts, fetched, p_near, dp_near, stats_near, stats_direct],
        18,
    )
    given = permuted(give, across_core)
    keep, ds_direct = local_call(
        keep_kernel,
        [((5 * block, head_dim), high), ((5 * tokens, rows), low)],
        [],
        [q_rows, do_rows, p_direct, dp_direct, shares],
        10,
    )
    back = given.astype(high)
    swapped = back[block : 2 * block]
    total_x = (keep[:block] + jnp.where(second == 0, swapped, 0.0)).astype(low)
    total_8 = jnp.concatenate(
        [
            keep[block : 2 * block] + jnp.where(second == 0, 0.0, swapped),
            keep[2 * block : 3 * block] + back[2 * block : 3 * block],
        ],
        axis=0,
    ).astype(low)
    total_4 = (keep[3 * block :] + back[3 * block :]).astype(low)
    back_4 = permuted(total_4, functools.partial(behind, 4))
    back_8 = permuted(total_8, functools.partial(behind, 8))
    back_x = permuted(total_x, across_x)
    grad_queries, mine = local_call(
        query_kernel,
        [(queries.shape, low), ((block, head_dim), high)],
        [((tokens, rows), low)],
        [q_rows, do_rows, p_near, dp_near, shares, ds_fetched, ds_direct, fetched, partner, by_x, by_8, by_4, own],
        13,
    )
    back_8, back_4, back_x, mine = lax.optimization_barrier((back_8, back_4, back_x, mine))
    far = back_8.astype(high) + back_4.astype(high)
    last = permuted(far[block:].astype(low), across_core)
    grad_keys, grad_values = local_call(
        result_kernel,
        [((tokens, head_dim), low)] * 2,
        [],
        [mine, given[:block], back_x, far, last],
        0,
    )
    return grad_queries, grad_keys, grad_values


def grouped(queries, keys, values, grad_out, doc_lengths):
    tokens, head_dim = keys.shape
    n_inner, n_outer = lax.axis_size("inner"), lax.axis_size("outer")

    def turned(value, steps):
        return lax.ppermute(
            value, "outer", [(at, (at + steps) % n_outer) for at in range(n_outer)]
        )

    own = jnp.concatenate([keys, values], axis=0)
    group = lax.all_gather(own, "inner", axis=0, tiled=True)
    pieces = [group] + [turned(group, step) for step in range(1, REACH + 1)]
    results = attend(
        functools.partial(grouped_slots, n_inner),
        functools.partial(grouped_slots, n_inner),
        REACH * n_inner,
        queries,
        grad_out,
        doc_lengths,
        pieces,
        [n_inner] * (REACH + 1),
        [jnp.float32] * (REACH + 1),
    )
    sums = results[1]
    for step in range(1, REACH + 1):
        sums = sums + turned(results[1 + step], -step)
    sums = lax.psum_scatter(sums, "inner", scatter_dimension=0, tiled=True)
    return (results[0],) + finish(sums, head_dim)


def on_device(queries, keys, values, grad_out, doc_lengths):
    if lax.axis_size("inner") == 2 and lax.axis_size("outer") % 4 == 0:
        return paired(queries, keys, values, grad_out, doc_lengths)
    return grouped(queries, keys, values, grad_out, doc_lengths)


def solution(mesh):
    rows = P(("outer", "inner"), None)
    return jax.shard_map(
        on_device,
        mesh=mesh,
        in_specs=(rows, rows, rows, rows, P()),
        out_specs=(rows, rows, rows),
        check_vma=False,
    )
```

```python
import functools
import math

import jax
import jax.numpy as jnp
from jax import lax
from jax.experimental import pallas as pl
from jax.experimental.pallas import tpu as pltpu
from jax.sharding import PartitionSpec as P

REACH = 4
NEG = -1e30
AXES = ("outer", "inner")
LANES_CONTRACT = (((1,), (1,)), ((), ()))
ROWS_CONTRACT = (((0,), (0,)), ((), ()))


def permuted(value, target):
    count = lax.axis_size("outer") * lax.axis_size("inner")
    return lax.ppermute(value, AXES, [(at, target(at, count)) for at in range(count)])


def across_core(at, count):
    return at ^ 2


def across_x(at, count):
    return at ^ 1


def ahead(steps, at, count):
    after = at + steps
    return after ^ ((at >> 1) & 1) if after < count else after - count


def behind(steps, at, count):
    before = at - steps
    return before ^ ((at >> 1) & 1) if before >= 0 else before + count


def own_slots(at):
    turned = at ^ ((at >> 1) & 1)
    slots = [at ^ 1]
    for steps in (8, 4):
        slots += [turned - steps, (turned ^ 2) - steps]
    return slots


def grouped_slots(n_inner, at):
    first = at - at % n_inner
    return [first - step * n_inner + j for step in range(REACH + 1) for j in range(n_inner)]


def attention_kernel(slots_of, given_of, window, heads, piece_blocks, out_blocks, docs, *refs):
    n_pieces, n_outs = len(piece_blocks), len(out_blocks)
    doc_ref, q_ref, do_ref = refs[:3]
    pieces = refs[3 : 3 + n_pieces]
    dq_ref = refs[3 + n_pieces]
    outs = refs[4 + n_pieces : 4 + n_pieces + n_outs]
    kw, vw, bias, t_buf, dp_buf, dk_acc, dv_acc = refs[4 + n_pieces + n_outs :]
    tokens, head_dim = q_ref.shape[0], kw.shape[1]
    n_inner = lax.axis_size("inner")
    me = lax.axis_index("outer") * n_inner + lax.axis_index("inner")
    slots = slots_of(me)
    scale = 1.0 / math.sqrt(head_dim)

    def rows_of(s):
        return pl.ds(pl.multiple_of(s * tokens, tokens), tokens)

    where = [(ref, i) for ref, n in zip(pieces, piece_blocks) for i in range(n)]
    for slot, (ref, i) in zip(slots, where):
        s = me - slot

        @pl.when((s >= 0) & (s <= window))
        def _():
            kw[rows_of(s), :] = ref[2 * i * tokens : (2 * i + 1) * tokens, :]
            vw[rows_of(s), :] = ref[(2 * i + 1) * tokens : (2 * i + 2) * tokens, :]

    position = me * tokens + lax.broadcasted_iota(jnp.int32, (1, tokens), 1)
    start = jnp.zeros((1, tokens), jnp.int32)
    end = jnp.int32(0)
    for n in range(docs):
        end = end + doc_ref[n]
        start = jnp.where(position >= end, end, start)
    for s in range(window + 1):
        key_at = (me - s) * tokens + lax.broadcasted_iota(jnp.int32, (tokens, tokens), 0)
        seen = (key_at >= start) & (key_at <= position)
        bias[s * tokens : (s + 1) * tokens, :] = jnp.where(seen, 0.0, NEG)

    factor = scale * math.log2(math.e)
    blocks = window + 1

    def one_pair(pair, slot, first):
        def side(ref):
            cut = [
                ref[:, pl.ds(pl.multiple_of((2 * pair + i) * head_dim, head_dim), head_dim)]
                for i in range(2)
            ]
            return jnp.concatenate(cut, axis=0)

        qp, dop = side(q_ref), side(do_ref)
        width = 2 * tokens
        peak = jnp.full((8, width), NEG, jnp.float32)
        for b in range(blocks):
            span = slice(b * tokens, (b + 1) * tokens)
            scores = lax.dot_general(
                kw[span, :], qp, LANES_CONTRACT, preferred_element_type=jnp.float32
            )
            off = bias[span, :]
            t = scores * factor + jnp.concatenate([off, off], axis=1)
            t_buf[slot, span, :] = t
            peak = jnp.maximum(peak, jnp.max(t.reshape(tokens // 8, 8, width), axis=0))
        peak = jnp.max(peak, axis=0, keepdims=True)
        total = jnp.zeros((8, width), jnp.float32)
        moment = jnp.zeros((8, width), jnp.float32)
        for b in range(blocks):
            span = slice(b * tokens, (b + 1) * tokens)
            p = jnp.exp2(t_buf[slot, span, :] - peak)
            dp = lax.dot_general(
                vw[span, :], dop, LANES_CONTRACT, preferred_element_type=jnp.float32
            )
            t_buf[slot, span, :] = p
            dp_buf[slot, span, :] = dp
            total = total + jnp.sum(p.reshape(tokens // 8, 8, width), axis=0)
            moment = moment + jnp.sum((p * dp).reshape(tokens // 8, 8, width), axis=0)
        share = 1.0 / jnp.sum(total, axis=0, keepdims=True)
        delta = jnp.sum(moment, axis=0, keepdims=True) * share
        dq = jnp.zeros((width, head_dim), jnp.float32)
        for b in range(blocks):
            span = slice(b * tokens, (b + 1) * tokens)
            p = t_buf[slot, span, :] * share
            low = p.astype(jnp.bfloat16)
            ds = (p * (dp_buf[slot, span, :] - delta)).astype(jnp.bfloat16)
            dv = jnp.dot(low, dop, preferred_element_type=jnp.float32)
            dk = jnp.dot(ds, qp, preferred_element_type=jnp.float32)
            if first is True:
                dv_acc[span, :] = dv
                dk_acc[span, :] = dk
            else:
                dv_acc[span, :] += dv
                dk_acc[span, :] += dk
            dq = dq + lax.dot_general(
                ds, kw[span, :], ROWS_CONTRACT, preferred_element_type=jnp.float32
            )
        dq = (dq * scale).astype(jnp.bfloat16)
        for i in range(2):
            dq_ref[:, pl.ds(pl.multiple_of((2 * pair + i) * head_dim, head_dim), head_dim)] = dq[
                i * tokens : (i + 1) * tokens
            ]

    n_pairs = heads // 2
    if blocks <= 12:
        for pair in range(n_pairs):
            one_pair(pair, pair % 2, pair == 0)
    else:
        dk_acc[...] = jnp.zeros_like(dk_acc)
        dv_acc[...] = jnp.zeros_like(dv_acc)

        def step(pair, carry):
            one_pair(pair, 0, False)
            return carry

        lax.fori_loop(0, n_pairs, step, 0)

    places = [(ref, i) for ref, n in zip(outs, out_blocks) for i in range(n)]
    for slot, (ref, i) in zip(given_of(me), places):
        s = me - slot
        first, second = (slice((2 * i + j) * tokens, (2 * i + j + 1) * tokens) for j in range(2))
        inside = (s >= 0) & (s <= window)

        @pl.when(inside)
        def _():
            ref[first, :] = dk_acc[rows_of(s), :].astype(ref.dtype)
            ref[second, :] = dv_acc[rows_of(s), :].astype(ref.dtype)

        @pl.when(jnp.logical_not(inside))
        def _():
            ref[first, :] = jnp.zeros((tokens, head_dim), ref.dtype)
            ref[second, :] = jnp.zeros((tokens, head_dim), ref.dtype)


def attend(slots_of, given_of, window, queries, grad_out, doc_lengths, pieces, out_blocks, out_types):
    tokens, width = queries.shape
    head_dim = pieces[0].shape[1]
    heads = width // head_dim
    keys = (window + 1) * tokens
    slots = 2 if window + 1 <= 12 else 1
    kernel = functools.partial(
        attention_kernel,
        slots_of,
        given_of,
        window,
        heads,
        [piece.shape[0] // (2 * tokens) for piece in pieces],
        out_blocks,
        doc_lengths.shape[0],
    )
    whole = pl.BlockSpec(memory_space=pltpu.VMEM)
    return pl.pallas_call(
        kernel,
        out_shape=[jax.ShapeDtypeStruct((tokens, width), jnp.bfloat16)]
        + [
            jax.ShapeDtypeStruct((2 * n * tokens, head_dim), kind)
            for n, kind in zip(out_blocks, out_types)
        ],
        in_specs=[pl.BlockSpec(memory_space=pltpu.SMEM)] + [whole] * (2 + len(pieces)),
        out_specs=[whole] * (1 + len(out_blocks)),
        scratch_shapes=[
            pltpu.VMEM((keys, head_dim), jnp.bfloat16),
            pltpu.VMEM((keys, head_dim), jnp.bfloat16),
            pltpu.VMEM((keys, tokens), jnp.float32),
            pltpu.VMEM((slots, keys, 2 * tokens), jnp.float32),
            pltpu.VMEM((slots, keys, 2 * tokens), jnp.float32),
            pltpu.VMEM((keys, head_dim), jnp.float32),
            pltpu.VMEM((keys, head_dim), jnp.float32),
        ],
        compiler_params=pltpu.CompilerParams(vmem_limit_bytes=(16 if window <= 12 else 56) * 2**20),
    )(doc_lengths, queries, grad_out, *pieces)


def finish(sums, head_dim):
    scale = 1.0 / math.sqrt(head_dim)
    half = sums.shape[0] // 2
    grad_keys = (sums[:half] * scale).astype(jnp.bfloat16)
    return grad_keys, sums[half:].astype(jnp.bfloat16)


def head_rows(ref, rows):
    tokens = ref.shape[0]
    head_dim = rows.shape[1]
    for h in range(rows.shape[0] // tokens):
        rows[h * tokens : (h + 1) * tokens, :] = ref[:, h * head_dim : (h + 1) * head_dim]


def own_position():
    return lax.axis_index("outer") * lax.axis_size("inner") + lax.axis_index("inner")


def document_starts(doc_ref, docs, position):
    start = jnp.zeros(position.shape, jnp.int32)
    end = jnp.int32(0)
    for n in range(docs):
        end = end + doc_ref[n]
        start = jnp.where(position >= end, end, start)
    return start


def by_reach(me, choices, body):
    for reached, chosen in zip((me >= 8, (me >= 4) & (me < 8), me < 4), choices):

        @pl.when(reached)
        def _():
            body(chosen)


def score_blocks(which, ids, blocks, start, me, q_rows, do_rows, bias, p_ref, dp_ref, stats):
    count = len(blocks)
    for b in range(count):
        if b not in which:
            stats[b : b + 1, :] = jnp.full((1, stats.shape[1]), NEG, jnp.float32)
            for kind in (1, 2):
                at = kind * count + b
                stats[at : at + 1, :] = jnp.zeros((1, stats.shape[1]), jnp.float32)
    if not which:
        return
    rows, head_dim = q_rows.shape
    tokens = bias.shape[1]
    factor = math.log2(math.e) / math.sqrt(head_dim)
    position = me * tokens + lax.broadcasted_iota(jnp.int32, (1, tokens), 1)
    spans = [slice(b * tokens, (b + 1) * tokens) for b in which]
    blocks = [blocks[b] for b in which]
    for span, at in zip(spans, [ids[b] for b in which]):
        key_at = at * tokens + lax.broadcasted_iota(jnp.int32, (tokens, tokens), 0)
        seen = (key_at >= start) & (key_at <= position)
        bias[span, :] = jnp.where(seen, 0.0, NEG)
    width = 2 * tokens
    parts = [[] for _ in blocks]
    for pair in range(rows // width):
        cols = slice(pair * width, (pair + 1) * width)
        qp, dop = q_rows[cols, :], do_rows[cols, :]
        for b, (span, found) in enumerate(zip(spans, parts)):
            if b % 4 == 0:
                group = blocks[b : b + 4]
                keys = jnp.concatenate([block[0]() for block in group], axis=0)
                values = jnp.concatenate([block[1]() for block in group], axis=0)
                scores_all = lax.dot_general(
                    keys, qp, LANES_CONTRACT, preferred_element_type=jnp.float32
                )
                dp_all = lax.dot_general(
                    values, dop, LANES_CONTRACT, preferred_element_type=jnp.float32
                )
            at = slice(b % 4 * tokens, (b % 4 + 1) * tokens)
            scores, dp = scores_all[at], dp_all[at]
            off = bias[span, :]
            t = scores * factor + jnp.concatenate([off, off], axis=1)
            peak = jnp.max(t, axis=0, keepdims=True)
            p = jnp.exp2(t - peak)
            p_ref[span, cols] = p
            dp_ref[span, cols] = dp
            total = jnp.sum(p, axis=0, keepdims=True)
            found.append((peak, total, jnp.sum(p * dp, axis=0, keepdims=True)))
    for b, found in zip(which, parts):
        for kind, values in enumerate(zip(*found)):
            at = kind * count + b
            stats[at : at + 1, :] = jnp.concatenate(values, axis=1)


def get_stats(ref, n):
    return [[ref[kind * n + b : kind * n + b + 1, :] for kind in range(3)] for b in range(n)]


def grad_blocks(which, reads, delta, q_rows, do_rows, ds_ref, put):
    head_dim = q_rows.shape[1]
    tokens = ds_ref.shape[0] // len(reads)
    for b in range(len(reads)):
        if b not in which:
            nothing = jnp.zeros((tokens, head_dim), jnp.float32)
            put(b, nothing, nothing)
    for start in range(0, len(which), 4):
        lows, all_ds = [], []
        for b in which[start : start + 4]:
            weights, dprobs, share = reads[b]
            p = weights() * share
            lows.append(p.astype(jnp.bfloat16))
            ds = (p * (dprobs() - delta)).astype(jnp.bfloat16)
            ds_ref[b * tokens : (b + 1) * tokens, :] = ds
            all_ds.append(ds)
        low, ds = jnp.concatenate(lows, axis=0), jnp.concatenate(all_ds, axis=0)
        dk = jnp.dot(ds, q_rows[...], preferred_element_type=jnp.float32)
        dv = jnp.dot(low, do_rows[...], preferred_element_type=jnp.float32)
        for i, b in enumerate(which[start : start + 4]):
            span = slice(i * tokens, (i + 1) * tokens)
            put(b, dk[span], dv[span])


def reads_of(p_ref, dp_ref, i, tokens, share):
    span = slice(i * tokens, (i + 1) * tokens)
    return (lambda: p_ref[span, :]), (lambda: dp_ref[span, :]), share


def block_of(ref, i, tokens):
    return (
        lambda: ref[2 * i * tokens : (2 * i + 1) * tokens, :],
        lambda: ref[(2 * i + 1) * tokens : (2 * i + 2) * tokens, :],
    )


def put_block(ref, i, dk, dv):
    tokens = dk.shape[0]
    ref[2 * i * tokens : (2 * i + 1) * tokens, :] = dk.astype(ref.dtype)
    ref[(2 * i + 1) * tokens : (2 * i + 2) * tokens, :] = dv.astype(ref.dtype)


def pack_kernel(keys, values, own, sems):
    tokens = keys.shape[0]
    copies = [
        pltpu.make_async_copy(ref, own.at[pl.ds(i * tokens, tokens), :], sems.at[i])
        for i, ref in enumerate((keys, values))
    ]
    for copy in copies:
        copy.start()
    for copy in copies:
        copy.wait()


def near_kernel(
    docs, doc_hbm, q_hbm, do_hbm, own, partner, by_x,
    p_out, dp_out, stats, q_rows, do_rows, starts,
    bias, doc_ref, sems,
):
    me = own_position()
    tokens = q_hbm.shape[0]
    rows, head_dim = q_rows.shape
    heads = rows // tokens
    copies = [pltpu.make_async_copy(doc_hbm, doc_ref, sems.at[2 * heads])]
    for i, (source, stacked) in enumerate(((q_hbm, q_rows), (do_hbm, do_rows))):
        for h in range(heads):
            copies.append(
                pltpu.make_async_copy(
                    source.at[:, pl.ds(h * head_dim, head_dim)],
                    stacked.at[pl.ds(h * tokens, tokens), :],
                    sems.at[i * heads + h],
                )
            )
    for copy in copies:
        copy.start()
    for copy in copies:
        copy.wait()
    position = me * tokens + lax.broadcasted_iota(jnp.int32, (1, tokens), 1)
    start = document_starts(doc_ref, docs, position)
    starts[0:1, :] = start
    score_blocks(
        (0, 1, 2),
        [me, me ^ 2, me ^ 1],
        [block_of(ref, 0, tokens) for ref in (own, partner, by_x)],
        start, me, q_rows, do_rows, bias, p_out, dp_out, stats,
    )


def direct_kernel(q_rows, do_rows, starts, by_8, by_4, p_out, dp_out, stats, bias):
    me = own_position()
    tokens = starts.shape[1]
    by_reach(
        me,
        ((0, 1, 2, 3), (2, 3), ()),
        lambda which: score_blocks(
            which,
            own_slots(me)[1:],
            [block_of(ref, i, tokens) for ref in (by_8, by_4) for i in range(2)],
            starts[0:1, :], me, q_rows, do_rows, bias, p_out, dp_out, stats,
        ),
    )


def fetched_ids(me):
    slots = own_slots(me ^ 2)
    return [jnp.where((me >> 1) & 1 == 0, slots[1], slots[0])] + slots[2:]


def fetched_kernel(
    q_rows, do_rows, starts, fetched, stats_near, stats_direct,
    give, ds_out, shares, bias, p_buf, dp_buf, stats,
):
    by_reach(
        own_position(),
        ((0, 1, 2, 3), (0, 2, 3), (0,)),
        lambda which: fetched_blocks(
            which, q_rows, do_rows, starts, fetched, stats_near, stats_direct,
            give, ds_out, shares, bias, p_buf, dp_buf, stats,
        ),
    )


def fetched_blocks(
    which, q_rows, do_rows, starts, fetched, stats_near, stats_direct,
    give, ds_out, shares, bias, p_buf, dp_buf, stats,
):
    me = own_position()
    tokens = starts.shape[1]
    score_blocks(
        which,
        fetched_ids(me),
        [block_of(fetched, i, tokens) for i in range(4)],
        starts[0:1, :], me, q_rows, do_rows, bias, p_buf, dp_buf, stats,
    )
    parts = get_stats(stats_near, 3) + get_stats(stats_direct, 4) + get_stats(stats, 4)
    top = functools.reduce(jnp.maximum, [part[0] for part in parts])
    factors = [jnp.exp2(part[0] - top) for part in parts]
    one = 1.0 / sum(f * part[1] for f, part in zip(factors, parts))
    delta = sum(f * part[2] for f, part in zip(factors, parts)) * one
    shared = [f * one for f in factors]
    for n in range(7):
        shares[n : n + 1, :] = shared[n]
    shares[7:8, :] = delta
    reads = [reads_of(p_buf, dp_buf, i, tokens, shared[7 + i]) for i in range(4)]
    grad_blocks(which, reads, delta, q_rows, do_rows, ds_out, functools.partial(put_block, give))


def keep_kernel(q_rows, do_rows, p_near, dp_near, p_direct, dp_direct, shares, keep, ds_out):
    tokens = p_near.shape[0] // 3
    delta = shares[7:8, :]
    places = [(p_near, dp_near, 2, 2)] + [(p_direct, dp_direct, 3 + i, i) for i in range(4)]
    reads = [
        reads_of(p_ref, dp_ref, i, tokens, shares[part : part + 1, :]) for p_ref, dp_ref, part, i in places
    ]
    by_reach(
        own_position(),
        ((0, 1, 2, 3, 4), (0, 3, 4), (0,)),
        lambda which: grad_blocks(which, reads, delta, q_rows, do_rows, ds_out, functools.partial(put_block, keep)),
    )


def query_kernel(
    q_rows, do_rows, p_ref, dp_ref, shares, ds_fetched, ds_direct, fetched, partner, by_x, by_8, by_4, own, back_x,
    dq_ref, mine, partners, ds_near,
):
    tokens = dq_ref.shape[0]
    head_dim = own.shape[1]
    scale = 1.0 / math.sqrt(head_dim)
    reads = [reads_of(p_ref, dp_ref, n, tokens, shares[n : n + 1, :]) for n in range(2)]
    grad_blocks(
        (0, 1), reads, shares[7:8, :], q_rows, do_rows, ds_near,
        lambda n, dk, dv: put_block((mine, partners)[n], 0, dk, dv),
    )
    mine[...] += back_x[...].astype(jnp.float32)
    where = [(ds_fetched, i, block_of(fetched, i, tokens)) for i in range(4)]
    direct = [(by_x, 0)] + [(ref, i) for ref in (by_8, by_4) for i in range(2)]
    where += [(ds_direct, n, block_of(ref, i, tokens)) for n, (ref, i) in enumerate(direct)]
    where += [(ds_near, n, block_of(ref, 0, tokens)) for n, ref in enumerate((own, partner))]
    by_reach(
        own_position(),
        (range(11), (0, 2, 3, 4, 7, 8, 9, 10), (0, 4, 9, 10)),
        lambda which: query_blocks([where[n] for n in which], dq_ref, scale),
    )


def query_blocks(where, dq_ref, scale):
    tokens, width = dq_ref.shape[0], 2 * dq_ref.shape[0]
    head_dim = where[0][2][0]().shape[1]
    for pair in range(dq_ref.shape[1] // (2 * head_dim)):
        cols = slice(pair * width, (pair + 1) * width)
        dq = jnp.zeros((width, head_dim), jnp.float32)
        for ref, n, (keys, values) in where:
            dq = dq + lax.dot_general(
                ref[n * tokens : (n + 1) * tokens, cols], keys(), ROWS_CONTRACT,
                preferred_element_type=jnp.float32,
            )
        dq = (dq * scale).astype(jnp.bfloat16)
        for i in range(2):
            h = 2 * pair + i
            dq_ref[:, h * head_dim : (h + 1) * head_dim] = dq[i * tokens : (i + 1) * tokens]


def result_kernel(mine, far, last, dk_ref, dv_ref):
    tokens, head_dim = dk_ref.shape
    for half, (ref, scale) in enumerate(((dk_ref, 1.0 / math.sqrt(head_dim)), (dv_ref, 1.0))):
        span = slice(half * tokens, (half + 1) * tokens)
        sums = mine[span, :] + far[span, :] + last[span, :].astype(jnp.float32)
        ref[...] = (sums * scale).astype(ref.dtype)


def local_call(kernel, outs, scratch, args, blocks, far=0):
    whole = pl.BlockSpec(memory_space=pltpu.VMEM)
    specs = [pl.BlockSpec(memory_space=pltpu.HBM)] * far + [whole] * (len(args) - far)
    return pl.pallas_call(
        kernel,
        out_shape=[jax.ShapeDtypeStruct(shape, kind) for shape, kind in outs],
        in_specs=specs,
        out_specs=[whole] * len(outs),
        scratch_shapes=[
            pltpu.VMEM(*entry) if isinstance(entry, tuple) else entry for entry in scratch
        ],
        compiler_params=pltpu.CompilerParams(vmem_limit_bytes=16 * 2**20),
        cost_estimate=pl.CostEstimate(
            flops=blocks * 2 * 128 * 128 * 1024, bytes_accessed=blocks * 2**19, transcendentals=0
        ),
    )(*[pltpu.with_memory_space_constraint(arg, pltpu.HBM) for arg in args[:far]], *args[far:])


def paired(queries, keys, values, grad_out, doc_lengths):
    tokens, head_dim = keys.shape
    low, high = jnp.bfloat16, jnp.float32
    block = 2 * tokens
    rows = queries.shape[1] // head_dim * tokens
    docs = doc_lengths.shape[0]
    second = (own_position() >> 1) & 1

    def part(n):
        return [((n * tokens, rows), high)] * 2 + [((16, rows), high)], [((n * tokens, tokens), high)]

    (own,) = local_call(
        pack_kernel, [((block, head_dim), low)], [pltpu.SemaphoreType.DMA((2,))], [keys, values], 0, far=2
    )
    partner = permuted(own, across_core)
    by_x = permuted(own, across_x)
    both = jnp.concatenate([own, partner], axis=0)
    by_4 = permuted(both, functools.partial(ahead, 4))
    by_8 = permuted(both, functools.partial(ahead, 8))
    outs, scratch = part(3)
    p_near, dp_near, stats_near, q_rows, do_rows, starts = local_call(
        functools.partial(near_kernel, docs),
        outs + [((rows, head_dim), low)] * 2 + [((8, tokens), jnp.int32)],
        scratch
        + [
            pltpu.SMEM(doc_lengths.shape, jnp.int32),
            pltpu.SemaphoreType.DMA((2 * (rows // tokens) + 1,)),
        ],
        [doc_lengths, queries, grad_out, own, partner, by_x],
        40,
        far=3,
    )
    by_8, by_4, stats_near = lax.optimization_barrier((by_8, by_4, stats_near))
    offered = jnp.where(second == 0, by_x, by_8[:block])
    fetched = permuted(jnp.concatenate([offered, by_8[block:], by_4], axis=0), across_core)
    p_direct, dp_direct, stats_direct = local_call(
        direct_kernel, *part(4), [q_rows, do_rows, starts, by_8, by_4], 8
    )
    give, ds_fetched, shares = local_call(
        fetched_kernel,
        [((4 * block, head_dim), low), ((4 * tokens, rows), low), ((8, rows), high)],
        part(4)[1] + [((4 * tokens, rows), high)] * 2 + [((16, rows), high)],
        [q_rows, do_rows, starts, fetched, stats_near, stats_direct],
        16,
    )
    given = permuted(give, across_core)
    keep, ds_direct = local_call(
        keep_kernel,
        [((5 * block, head_dim), high), ((5 * tokens, rows), low)],
        [],
        [q_rows, do_rows, p_near, dp_near, p_direct, dp_direct, shares],
        10,
    )
    back = given.astype(high)
    swapped = back[:block]
    total_x = (keep[:block] + jnp.where(second == 0, swapped, 0.0)).astype(low)
    total_8 = jnp.concatenate(
        [
            keep[block : 2 * block] + jnp.where(second == 0, 0.0, swapped),
            keep[2 * block : 3 * block] + back[block : 2 * block],
        ],
        axis=0,
    ).astype(low)
    total_4 = (keep[3 * block :] + back[2 * block :]).astype(low)
    back_4 = permuted(total_4, functools.partial(behind, 4))
    back_8 = permuted(total_8, functools.partial(behind, 8))
    back_x = permuted(total_x, across_x)
    grad_queries, mine, partners = local_call(
        query_kernel,
        [(queries.shape, low)] + [((block, head_dim), high)] * 2,
        [((2 * tokens, rows), low)],
        [
            q_rows, do_rows, p_near, dp_near, shares, ds_fetched, ds_direct,
            fetched, partner, by_x, by_8, by_4, own, back_x,
        ],
        40,
    )
    far = back_8.astype(high) + back_4.astype(high)
    last = permuted((far[block:] + partners).astype(low), across_core)
    grad_keys, grad_values = local_call(
        result_kernel,
        [((tokens, head_dim), low)] * 2,
        [],
        [mine, far, last],
        0,
    )
    return grad_queries, grad_keys, grad_values


def grouped(queries, keys, values, grad_out, doc_lengths):
    tokens, head_dim = keys.shape
    n_inner, n_outer = lax.axis_size("inner"), lax.axis_size("outer")

    def turned(value, steps):
        return lax.ppermute(
            value, "outer", [(at, (at + steps) % n_outer) for at in range(n_outer)]
        )

    own = jnp.concatenate([keys, values], axis=0)
    group = lax.all_gather(own, "inner", axis=0, tiled=True)
    pieces = [group] + [turned(group, step) for step in range(1, REACH + 1)]
    results = attend(
        functools.partial(grouped_slots, n_inner),
        functools.partial(grouped_slots, n_inner),
        REACH * n_inner,
        queries,
        grad_out,
        doc_lengths,
        pieces,
        [n_inner] * (REACH + 1),
        [jnp.float32] * (REACH + 1),
    )
    sums = results[1]
    for step in range(1, REACH + 1):
        sums = sums + turned(results[1 + step], -step)
    sums = lax.psum_scatter(sums, "inner", scatter_dimension=0, tiled=True)
    return (results[0],) + finish(sums, head_dim)


def on_device(queries, keys, values, grad_out, doc_lengths):
    if lax.axis_size("inner") == 2 and lax.axis_size("outer") % 4 == 0:
        return paired(queries, keys, values, grad_out, doc_lengths)
    return grouped(queries, keys, values, grad_out, doc_lengths)


def solution(mesh):
    rows = P(("outer", "inner"), None)
    return jax.shard_map(
        on_device,
        mesh=mesh,
        in_specs=(rows, rows, rows, rows, P()),
        out_specs=(rows, rows, rows),
        check_vma=False,
    )
```

```python
import functools
import math

import jax
import jax.numpy as jnp
from jax import lax
from jax.experimental import pallas as pl
from jax.experimental.pallas import tpu as pltpu
from jax.sharding import PartitionSpec as P

REACH = 4
NEG = -1e30
AXES = ("outer", "inner")
LANES_CONTRACT = (((1,), (1,)), ((), ()))
ROWS_CONTRACT = (((0,), (0,)), ((), ()))


def permuted(value, target):
    count = lax.axis_size("outer") * lax.axis_size("inner")
    return lax.ppermute(value, AXES, [(at, target(at, count)) for at in range(count)])


def across_core(at, count):
    return at ^ 2


def across_x(at, count):
    return at ^ 1


def ahead(steps, at, count):
    after = at + steps
    return after ^ ((at >> 1) & 1) if after < count else after - count


def behind(steps, at, count):
    before = at - steps
    return before ^ ((at >> 1) & 1) if before >= 0 else before + count


def own_slots(at):
    turned = at ^ ((at >> 1) & 1)
    slots = [at ^ 1]
    for steps in (8, 4):
        slots += [turned - steps, (turned ^ 2) - steps]
    return slots


def grouped_slots(n_inner, at):
    first = at - at % n_inner
    return [first - step * n_inner + j for step in range(REACH + 1) for j in range(n_inner)]


def attention_kernel(slots_of, given_of, window, heads, piece_blocks, out_blocks, docs, *refs):
    n_pieces, n_outs = len(piece_blocks), len(out_blocks)
    doc_ref, q_ref, do_ref = refs[:3]
    pieces = refs[3 : 3 + n_pieces]
    dq_ref = refs[3 + n_pieces]
    outs = refs[4 + n_pieces : 4 + n_pieces + n_outs]
    kw, vw, bias, t_buf, dp_buf, dk_acc, dv_acc = refs[4 + n_pieces + n_outs :]
    tokens, head_dim = q_ref.shape[0], kw.shape[1]
    n_inner = lax.axis_size("inner")
    me = lax.axis_index("outer") * n_inner + lax.axis_index("inner")
    slots = slots_of(me)
    scale = 1.0 / math.sqrt(head_dim)

    def rows_of(s):
        return pl.ds(pl.multiple_of(s * tokens, tokens), tokens)

    where = [(ref, i) for ref, n in zip(pieces, piece_blocks) for i in range(n)]
    for slot, (ref, i) in zip(slots, where):
        s = me - slot

        @pl.when((s >= 0) & (s <= window))
        def _():
            kw[rows_of(s), :] = ref[2 * i * tokens : (2 * i + 1) * tokens, :]
            vw[rows_of(s), :] = ref[(2 * i + 1) * tokens : (2 * i + 2) * tokens, :]

    position = me * tokens + lax.broadcasted_iota(jnp.int32, (1, tokens), 1)
    start = jnp.zeros((1, tokens), jnp.int32)
    end = jnp.int32(0)
    for n in range(docs):
        end = end + doc_ref[n]
        start = jnp.where(position >= end, end, start)
    for s in range(window + 1):
        key_at = (me - s) * tokens + lax.broadcasted_iota(jnp.int32, (tokens, tokens), 0)
        seen = (key_at >= start) & (key_at <= position)
        bias[s * tokens : (s + 1) * tokens, :] = jnp.where(seen, 0.0, NEG)

    factor = scale * math.log2(math.e)
    blocks = window + 1

    def one_pair(pair, slot, first):
        def side(ref):
            cut = [
                ref[:, pl.ds(pl.multiple_of((2 * pair + i) * head_dim, head_dim), head_dim)]
                for i in range(2)
            ]
            return jnp.concatenate(cut, axis=0)

        qp, dop = side(q_ref), side(do_ref)
        width = 2 * tokens
        peak = jnp.full((8, width), NEG, jnp.float32)
        for b in range(blocks):
            span = slice(b * tokens, (b + 1) * tokens)
            scores = lax.dot_general(
                kw[span, :], qp, LANES_CONTRACT, preferred_element_type=jnp.float32
            )
            off = bias[span, :]
            t = scores * factor + jnp.concatenate([off, off], axis=1)
            t_buf[slot, span, :] = t
            peak = jnp.maximum(peak, jnp.max(t.reshape(tokens // 8, 8, width), axis=0))
        peak = jnp.max(peak, axis=0, keepdims=True)
        total = jnp.zeros((8, width), jnp.float32)
        moment = jnp.zeros((8, width), jnp.float32)
        for b in range(blocks):
            span = slice(b * tokens, (b + 1) * tokens)
            p = jnp.exp2(t_buf[slot, span, :] - peak)
            dp = lax.dot_general(
                vw[span, :], dop, LANES_CONTRACT, preferred_element_type=jnp.float32
            )
            t_buf[slot, span, :] = p
            dp_buf[slot, span, :] = dp
            total = total + jnp.sum(p.reshape(tokens // 8, 8, width), axis=0)
            moment = moment + jnp.sum((p * dp).reshape(tokens // 8, 8, width), axis=0)
        share = 1.0 / jnp.sum(total, axis=0, keepdims=True)
        delta = jnp.sum(moment, axis=0, keepdims=True) * share
        dq = jnp.zeros((width, head_dim), jnp.float32)
        for b in range(blocks):
            span = slice(b * tokens, (b + 1) * tokens)
            p = t_buf[slot, span, :] * share
            low = p.astype(jnp.bfloat16)
            ds = (p * (dp_buf[slot, span, :] - delta)).astype(jnp.bfloat16)
            dv = jnp.dot(low, dop, preferred_element_type=jnp.float32)
            dk = jnp.dot(ds, qp, preferred_element_type=jnp.float32)
            if first is True:
                dv_acc[span, :] = dv
                dk_acc[span, :] = dk
            else:
                dv_acc[span, :] += dv
                dk_acc[span, :] += dk
            dq = dq + lax.dot_general(
                ds, kw[span, :], ROWS_CONTRACT, preferred_element_type=jnp.float32
            )
        dq = (dq * scale).astype(jnp.bfloat16)
        for i in range(2):
            dq_ref[:, pl.ds(pl.multiple_of((2 * pair + i) * head_dim, head_dim), head_dim)] = dq[
                i * tokens : (i + 1) * tokens
            ]

    n_pairs = heads // 2
    if blocks <= 12:
        for pair in range(n_pairs):
            one_pair(pair, pair % 2, pair == 0)
    else:
        dk_acc[...] = jnp.zeros_like(dk_acc)
        dv_acc[...] = jnp.zeros_like(dv_acc)

        def step(pair, carry):
            one_pair(pair, 0, False)
            return carry

        lax.fori_loop(0, n_pairs, step, 0)

    places = [(ref, i) for ref, n in zip(outs, out_blocks) for i in range(n)]
    for slot, (ref, i) in zip(given_of(me), places):
        s = me - slot
        first, second = (slice((2 * i + j) * tokens, (2 * i + j + 1) * tokens) for j in range(2))
        inside = (s >= 0) & (s <= window)

        @pl.when(inside)
        def _():
            ref[first, :] = dk_acc[rows_of(s), :].astype(ref.dtype)
            ref[second, :] = dv_acc[rows_of(s), :].astype(ref.dtype)

        @pl.when(jnp.logical_not(inside))
        def _():
            ref[first, :] = jnp.zeros((tokens, head_dim), ref.dtype)
            ref[second, :] = jnp.zeros((tokens, head_dim), ref.dtype)


def attend(slots_of, given_of, window, queries, grad_out, doc_lengths, pieces, out_blocks, out_types):
    tokens, width = queries.shape
    head_dim = pieces[0].shape[1]
    heads = width // head_dim
    keys = (window + 1) * tokens
    slots = 2 if window + 1 <= 12 else 1
    kernel = functools.partial(
        attention_kernel,
        slots_of,
        given_of,
        window,
        heads,
        [piece.shape[0] // (2 * tokens) for piece in pieces],
        out_blocks,
        doc_lengths.shape[0],
    )
    whole = pl.BlockSpec(memory_space=pltpu.VMEM)
    return pl.pallas_call(
        kernel,
        out_shape=[jax.ShapeDtypeStruct((tokens, width), jnp.bfloat16)]
        + [
            jax.ShapeDtypeStruct((2 * n * tokens, head_dim), kind)
            for n, kind in zip(out_blocks, out_types)
        ],
        in_specs=[pl.BlockSpec(memory_space=pltpu.SMEM)] + [whole] * (2 + len(pieces)),
        out_specs=[whole] * (1 + len(out_blocks)),
        scratch_shapes=[
            pltpu.VMEM((keys, head_dim), jnp.bfloat16),
            pltpu.VMEM((keys, head_dim), jnp.bfloat16),
            pltpu.VMEM((keys, tokens), jnp.float32),
            pltpu.VMEM((slots, keys, 2 * tokens), jnp.float32),
            pltpu.VMEM((slots, keys, 2 * tokens), jnp.float32),
            pltpu.VMEM((keys, head_dim), jnp.float32),
            pltpu.VMEM((keys, head_dim), jnp.float32),
        ],
        compiler_params=pltpu.CompilerParams(vmem_limit_bytes=(16 if window <= 12 else 56) * 2**20),
    )(doc_lengths, queries, grad_out, *pieces)


def finish(sums, head_dim):
    scale = 1.0 / math.sqrt(head_dim)
    half = sums.shape[0] // 2
    grad_keys = (sums[:half] * scale).astype(jnp.bfloat16)
    return grad_keys, sums[half:].astype(jnp.bfloat16)


def head_rows(ref, rows):
    tokens = ref.shape[0]
    head_dim = rows.shape[1]
    for h in range(rows.shape[0] // tokens):
        rows[h * tokens : (h + 1) * tokens, :] = ref[:, h * head_dim : (h + 1) * head_dim]


def own_position():
    return lax.axis_index("outer") * lax.axis_size("inner") + lax.axis_index("inner")


def document_starts(doc_ref, docs, position):
    start = jnp.zeros(position.shape, jnp.int32)
    end = jnp.int32(0)
    for n in range(docs):
        end = end + doc_ref[n]
        start = jnp.where(position >= end, end, start)
    return start


def by_reach(me, choices, body):
    for reached, chosen in zip((me >= 8, (me >= 4) & (me < 8), me < 4), choices):

        @pl.when(reached)
        def _():
            body(chosen)


def score_blocks(which, ids, blocks, start, me, q_rows, do_rows, bias, p_ref, dp_ref, stats):
    count = len(blocks)
    for b in range(count):
        if b not in which:
            stats[b : b + 1, :] = jnp.full((1, stats.shape[1]), NEG, jnp.float32)
            for kind in (1, 2):
                at = kind * count + b
                stats[at : at + 1, :] = jnp.zeros((1, stats.shape[1]), jnp.float32)
    if not which:
        return
    rows, head_dim = q_rows.shape
    tokens = bias.shape[1]
    factor = math.log2(math.e) / math.sqrt(head_dim)
    position = me * tokens + lax.broadcasted_iota(jnp.int32, (1, tokens), 1)
    spans = [slice(b * tokens, (b + 1) * tokens) for b in which]
    blocks = [blocks[b] for b in which]
    for span, at in zip(spans, [ids[b] for b in which]):
        key_at = at * tokens + lax.broadcasted_iota(jnp.int32, (tokens, tokens), 0)
        seen = (key_at >= start) & (key_at <= position)
        bias[span, :] = jnp.where(seen, 0.0, NEG)
    width = 2 * tokens
    parts = [[] for _ in blocks]
    for pair in range(rows // width):
        cols = slice(pair * width, (pair + 1) * width)
        qp, dop = q_rows[cols, :], do_rows[cols, :]
        for b, (span, found) in enumerate(zip(spans, parts)):
            if b % 4 == 0:
                group = blocks[b : b + 4]
                keys = jnp.concatenate([block[0]() for block in group], axis=0)
                values = jnp.concatenate([block[1]() for block in group], axis=0)
                scores_all = lax.dot_general(
                    keys, qp, LANES_CONTRACT, preferred_element_type=jnp.float32
                )
                dp_all = lax.dot_general(
                    values, dop, LANES_CONTRACT, preferred_element_type=jnp.float32
                )
            at = slice(b % 4 * tokens, (b % 4 + 1) * tokens)
            scores, dp = scores_all[at], dp_all[at]
            off = bias[span, :]
            t = scores * factor + jnp.concatenate([off, off], axis=1)
            peak = jnp.max(t, axis=0, keepdims=True)
            p = jnp.exp2(t - peak)
            p_ref[span, cols] = p
            dp_ref[span, cols] = dp
            total = jnp.sum(p, axis=0, keepdims=True)
            found.append((peak, total, jnp.sum(p * dp, axis=0, keepdims=True)))
    for b, found in zip(which, parts):
        for kind, values in enumerate(zip(*found)):
            at = kind * count + b
            stats[at : at + 1, :] = jnp.concatenate(values, axis=1)


def get_stats(ref, n):
    return [[ref[kind * n + b : kind * n + b + 1, :] for kind in range(3)] for b in range(n)]


def grad_blocks(which, reads, delta, q_rows, do_rows, ds_ref, put):
    head_dim = q_rows.shape[1]
    tokens = ds_ref.shape[0] // len(reads)
    for b in range(len(reads)):
        if b not in which:
            nothing = jnp.zeros((tokens, head_dim), jnp.float32)
            put(b, nothing, nothing)
    for start in range(0, len(which), 4):
        lows, all_ds = [], []
        for b in which[start : start + 4]:
            weights, dprobs, share = reads[b]
            p = weights() * share
            lows.append(p.astype(jnp.bfloat16))
            ds = (p * (dprobs() - delta)).astype(jnp.bfloat16)
            ds_ref[b * tokens : (b + 1) * tokens, :] = ds
            all_ds.append(ds)
        low, ds = jnp.concatenate(lows, axis=0), jnp.concatenate(all_ds, axis=0)
        dk = jnp.dot(ds, q_rows[...], preferred_element_type=jnp.float32)
        dv = jnp.dot(low, do_rows[...], preferred_element_type=jnp.float32)
        for i, b in enumerate(which[start : start + 4]):
            span = slice(i * tokens, (i + 1) * tokens)
            put(b, dk[span], dv[span])


def reads_of(p_ref, dp_ref, i, tokens, share):
    span = slice(i * tokens, (i + 1) * tokens)
    return (lambda: p_ref[span, :]), (lambda: dp_ref[span, :]), share


def block_of(ref, i, tokens):
    return (
        lambda: ref[2 * i * tokens : (2 * i + 1) * tokens, :],
        lambda: ref[(2 * i + 1) * tokens : (2 * i + 2) * tokens, :],
    )


def put_block(ref, i, dk, dv):
    tokens = dk.shape[0]
    ref[2 * i * tokens : (2 * i + 1) * tokens, :] = dk.astype(ref.dtype)
    ref[(2 * i + 1) * tokens : (2 * i + 2) * tokens, :] = dv.astype(ref.dtype)


def pack_kernel(keys, values, own, sems):
    tokens = keys.shape[0]
    copies = [
        pltpu.make_async_copy(ref, own.at[pl.ds(i * tokens, tokens), :], sems.at[i])
        for i, ref in enumerate((keys, values))
    ]
    for copy in copies:
        copy.start()
    for copy in copies:
        copy.wait()


def near_kernel(
    docs, doc_hbm, q_hbm, do_hbm, own, partner, by_x,
    p_out, dp_out, stats, q_rows, do_rows, starts,
    bias, doc_ref, sems,
):
    me = own_position()
    tokens = q_hbm.shape[0]
    rows, head_dim = q_rows.shape
    heads = rows // tokens
    copies = [pltpu.make_async_copy(doc_hbm, doc_ref, sems.at[2 * heads])]
    for i, (source, stacked) in enumerate(((q_hbm, q_rows), (do_hbm, do_rows))):
        for h in range(heads):
            copies.append(
                pltpu.make_async_copy(
                    source.at[:, pl.ds(h * head_dim, head_dim)],
                    stacked.at[pl.ds(h * tokens, tokens), :],
                    sems.at[i * heads + h],
                )
            )
    for copy in copies:
        copy.start()
    for copy in copies:
        copy.wait()
    position = me * tokens + lax.broadcasted_iota(jnp.int32, (1, tokens), 1)
    start = document_starts(doc_ref, docs, position)
    starts[0:1, :] = start
    score_blocks(
        (0, 1, 2),
        [me, me ^ 2, me ^ 1],
        [block_of(ref, 0, tokens) for ref in (own, partner, by_x)],
        start, me, q_rows, do_rows, bias, p_out, dp_out, stats,
    )


def direct_kernel(q_rows, do_rows, starts, by_8, by_4, p_out, dp_out, stats, bias):
    me = own_position()
    tokens = starts.shape[1]
    by_reach(
        me,
        ((0, 1, 2, 3), (2, 3), ()),
        lambda which: score_blocks(
            which,
            own_slots(me)[1:],
            [block_of(ref, i, tokens) for ref in (by_8, by_4) for i in range(2)],
            starts[0:1, :], me, q_rows, do_rows, bias, p_out, dp_out, stats,
        ),
    )


def fetched_ids(me):
    slots = own_slots(me ^ 2)
    return [jnp.where((me >> 1) & 1 == 0, slots[1], slots[0])] + slots[2:]


def fetched_kernel(
    q_rows, do_rows, starts, fetched, stats_near, stats_direct,
    give, ds_out, shares, bias, p_buf, dp_buf, stats,
):
    by_reach(
        own_position(),
        ((0, 1, 2, 3), (0, 2, 3), (0,)),
        lambda which: fetched_blocks(
            which, q_rows, do_rows, starts, fetched, stats_near, stats_direct,
            give, ds_out, shares, bias, p_buf, dp_buf, stats,
        ),
    )


def fetched_blocks(
    which, q_rows, do_rows, starts, fetched, stats_near, stats_direct,
    give, ds_out, shares, bias, p_buf, dp_buf, stats,
):
    me = own_position()
    tokens = starts.shape[1]
    score_blocks(
        which,
        fetched_ids(me),
        [block_of(fetched, i, tokens) for i in range(4)],
        starts[0:1, :], me, q_rows, do_rows, bias, p_buf, dp_buf, stats,
    )
    parts = get_stats(stats_near, 3) + get_stats(stats_direct, 4) + get_stats(stats, 4)
    top = functools.reduce(jnp.maximum, [part[0] for part in parts])
    factors = [jnp.exp2(part[0] - top) for part in parts]
    one = 1.0 / sum(f * part[1] for f, part in zip(factors, parts))
    delta = sum(f * part[2] for f, part in zip(factors, parts)) * one
    shared = [f * one for f in factors]
    for n in range(7):
        shares[n : n + 1, :] = shared[n]
    shares[7:8, :] = delta
    reads = [reads_of(p_buf, dp_buf, i, tokens, shared[7 + i]) for i in range(4)]
    grad_blocks(which, reads, delta, q_rows, do_rows, ds_out, functools.partial(put_block, give))


def keep_kernel(q_rows, do_rows, p_near, dp_near, p_direct, dp_direct, shares, keep, ds_out):
    tokens = p_near.shape[0] // 3
    delta = shares[7:8, :]
    places = [(p_near, dp_near, 2, 2)] + [(p_direct, dp_direct, 3 + i, i) for i in range(4)]
    reads = [
        reads_of(p_ref, dp_ref, i, tokens, shares[part : part + 1, :]) for p_ref, dp_ref, part, i in places
    ]
    by_reach(
        own_position(),
        ((0, 1, 2, 3, 4), (0, 3, 4), (0,)),
        lambda which: grad_blocks(which, reads, delta, q_rows, do_rows, ds_out, functools.partial(put_block, keep)),
    )


def query_kernel(
    q_rows, do_rows, p_ref, dp_ref, shares, ds_fetched, ds_direct, fetched, partner, by_x, by_8, by_4, own, back_x,
    dq_ref, mine, partners, ds_near,
):
    tokens = dq_ref.shape[0]
    head_dim = own.shape[1]
    scale = 1.0 / math.sqrt(head_dim)
    reads = [reads_of(p_ref, dp_ref, n, tokens, shares[n : n + 1, :]) for n in range(2)]
    grad_blocks(
        (0, 1), reads, shares[7:8, :], q_rows, do_rows, ds_near,
        lambda n, dk, dv: put_block((mine, partners)[n], 0, dk, dv),
    )
    mine[...] += back_x[...].astype(jnp.float32)
    where = [(ds_fetched, i, block_of(fetched, i, tokens)) for i in range(4)]
    direct = [(by_x, 0)] + [(ref, i) for ref in (by_8, by_4) for i in range(2)]
    where += [(ds_direct, n, block_of(ref, i, tokens)) for n, (ref, i) in enumerate(direct)]
    where += [(ds_near, n, block_of(ref, 0, tokens)) for n, ref in enumerate((own, partner))]
    by_reach(
        own_position(),
        (range(11), (0, 2, 3, 4, 7, 8, 9, 10), (0, 4, 9, 10)),
        lambda which: query_blocks([where[n] for n in which], dq_ref, scale),
    )


def query_blocks(where, dq_ref, scale):
    tokens, width = dq_ref.shape[0], 2 * dq_ref.shape[0]
    head_dim = where[0][2][0]().shape[1]
    for pair in range(dq_ref.shape[1] // (2 * head_dim)):
        cols = slice(pair * width, (pair + 1) * width)
        dq = jnp.zeros((width, head_dim), jnp.float32)
        for ref, n, (keys, values) in where:
            dq = dq + lax.dot_general(
                ref[n * tokens : (n + 1) * tokens, cols], keys(), ROWS_CONTRACT,
                preferred_element_type=jnp.float32,
            )
        dq = (dq * scale).astype(jnp.bfloat16)
        for i in range(2):
            h = 2 * pair + i
            dq_ref[:, h * head_dim : (h + 1) * head_dim] = dq[i * tokens : (i + 1) * tokens]


def result_kernel(mine, far, last, dk_ref, dv_ref):
    tokens, head_dim = dk_ref.shape
    for half, (ref, scale) in enumerate(((dk_ref, 1.0 / math.sqrt(head_dim)), (dv_ref, 1.0))):
        span = slice(half * tokens, (half + 1) * tokens)
        sums = mine[span, :] + far[span, :] + last[span, :].astype(jnp.float32)
        ref[...] = (sums * scale).astype(ref.dtype)


def local_call(kernel, outs, scratch, args, blocks, far=0):
    whole = pl.BlockSpec(memory_space=pltpu.VMEM)
    specs = [pl.BlockSpec(memory_space=pltpu.HBM)] * far + [whole] * (len(args) - far)
    return pl.pallas_call(
        kernel,
        out_shape=[jax.ShapeDtypeStruct(shape, kind) for shape, kind in outs],
        in_specs=specs,
        out_specs=[whole] * len(outs),
        scratch_shapes=[
            pltpu.VMEM(*entry) if isinstance(entry, tuple) else entry for entry in scratch
        ],
        compiler_params=pltpu.CompilerParams(vmem_limit_bytes=16 * 2**20),
        cost_estimate=pl.CostEstimate(
            flops=blocks * 2 * 128 * 128 * 1024, bytes_accessed=blocks * 2**19, transcendentals=0
        ),
    )(*[pltpu.with_memory_space_constraint(arg, pltpu.HBM) for arg in args[:far]], *args[far:])


def paired(queries, keys, values, grad_out, doc_lengths):
    tokens, head_dim = keys.shape
    low, high = jnp.bfloat16, jnp.float32
    block = 2 * tokens
    rows = queries.shape[1] // head_dim * tokens
    docs = doc_lengths.shape[0]
    second = (own_position() >> 1) & 1

    def part(n):
        return [((n * tokens, rows), high)] * 2 + [((16, rows), high)], [((n * tokens, tokens), high)]

    (own,) = local_call(
        pack_kernel, [((block, head_dim), low)], [pltpu.SemaphoreType.DMA((2,))], [keys, values], 0, far=2
    )
    partner = permuted(own, across_core)
    by_x = permuted(own, across_x)
    both = jnp.concatenate([own, partner], axis=0)
    by_4 = permuted(both, functools.partial(ahead, 4))
    by_8 = jnp.concatenate([permuted(own, functools.partial(ahead, 8)), permuted(partner, functools.partial(ahead, 8))], axis=0)
    outs, scratch = part(3)
    p_near, dp_near, stats_near, q_rows, do_rows, starts = local_call(
        functools.partial(near_kernel, docs),
        outs + [((rows, head_dim), low)] * 2 + [((8, tokens), jnp.int32)],
        scratch
        + [
            pltpu.SMEM(doc_lengths.shape, jnp.int32),
            pltpu.SemaphoreType.DMA((2 * (rows // tokens) + 1,)),
        ],
        [doc_lengths, queries, grad_out, own, partner, by_x],
        40,
        far=3,
    )
    by_8, by_4, stats_near = lax.optimization_barrier((by_8, by_4, stats_near))
    offered = jnp.where(second == 0, by_x, by_8[:block])
    fetched = permuted(jnp.concatenate([offered, by_8[block:], by_4], axis=0), across_core)
    p_direct, dp_direct, stats_direct = local_call(
        direct_kernel, *part(4), [q_rows, do_rows, starts, by_8, by_4], 8
    )
    give, ds_fetched, shares = local_call(
        fetched_kernel,
        [((4 * block, head_dim), low), ((4 * tokens, rows), low), ((8, rows), high)],
        part(4)[1] + [((4 * tokens, rows), high)] * 2 + [((16, rows), high)],
        [q_rows, do_rows, starts, fetched, stats_near, stats_direct],
        16,
    )
    given = permuted(give, across_core)
    keep, ds_direct = local_call(
        keep_kernel,
        [((5 * block, head_dim), high), ((5 * tokens, rows), low)],
        [],
        [q_rows, do_rows, p_near, dp_near, p_direct, dp_direct, shares],
        10,
    )
    back = given.astype(high)
    swapped = back[:block]
    total_x = (keep[:block] + jnp.where(second == 0, swapped, 0.0)).astype(low)
    total_8 = jnp.concatenate(
        [
            keep[block : 2 * block] + jnp.where(second == 0, 0.0, swapped),
            keep[2 * block : 3 * block] + back[block : 2 * block],
        ],
        axis=0,
    ).astype(low)
    total_4 = (keep[3 * block :] + back[2 * block :]).astype(low)
    back_4 = permuted(total_4, functools.partial(behind, 4))
    back_8 = permuted(total_8, functools.partial(behind, 8))
    back_x = permuted(total_x, across_x)
    grad_queries, mine, partners = local_call(
        query_kernel,
        [(queries.shape, low)] + [((block, head_dim), high)] * 2,
        [((2 * tokens, rows), low)],
        [
            q_rows, do_rows, p_near, dp_near, shares, ds_fetched, ds_direct,
            fetched, partner, by_x, by_8, by_4, own, back_x,
        ],
        40,
    )
    far = back_8.astype(high) + back_4.astype(high)
    last = permuted((far[block:] + partners).astype(low), across_core)
    grad_keys, grad_values = local_call(
        result_kernel,
        [((tokens, head_dim), low)] * 2,
        [],
        [mine, far, last],
        0,
    )
    return grad_queries, grad_keys, grad_values


def grouped(queries, keys, values, grad_out, doc_lengths):
    tokens, head_dim = keys.shape
    n_inner, n_outer = lax.axis_size("inner"), lax.axis_size("outer")

    def turned(value, steps):
        return lax.ppermute(
            value, "outer", [(at, (at + steps) % n_outer) for at in range(n_outer)]
        )

    own = jnp.concatenate([keys, values], axis=0)
    group = lax.all_gather(own, "inner", axis=0, tiled=True)
    pieces = [group] + [turned(group, step) for step in range(1, REACH + 1)]
    results = attend(
        functools.partial(grouped_slots, n_inner),
        functools.partial(grouped_slots, n_inner),
        REACH * n_inner,
        queries,
        grad_out,
        doc_lengths,
        pieces,
        [n_inner] * (REACH + 1),
        [jnp.float32] * (REACH + 1),
    )
    sums = results[1]
    for step in range(1, REACH + 1):
        sums = sums + turned(results[1 + step], -step)
    sums = lax.psum_scatter(sums, "inner", scatter_dimension=0, tiled=True)
    return (results[0],) + finish(sums, head_dim)


def on_device(queries, keys, values, grad_out, doc_lengths):
    if lax.axis_size("inner") == 2 and lax.axis_size("outer") % 4 == 0:
        return paired(queries, keys, values, grad_out, doc_lengths)
    return grouped(queries, keys, values, grad_out, doc_lengths)


def solution(mesh):
    rows = P(("outer", "inner"), None)
    return jax.shard_map(
        on_device,
        mesh=mesh,
        in_specs=(rows, rows, rows, rows, P()),
        out_specs=(rows, rows, rows),
        check_vma=False,
    )
```
